32 devices in a mesh: dp: 16 (over z, y, core), seq: 2 (over x).
Axes of the slice: x: 2, y: 2, z: 4, core: 2. Of those that a mesh axis runs over, the one named last changes fastest.
Arguments:
- tokens: bfloat16 [32, 1024, 1024], P('dp', 'seq'), may hold values from -6 to 6
- cotangent: bfloat16 [32, 1024, 1024], P('dp', 'seq'), may hold values from -6 to 6
- segments: int32 [32, 1024], P('dp'), may hold values from 0 to 3, as said below
- global_blocks: int32 [32, 2], P('dp'), may hold values from 0 to 15, as said below
- random_blocks: int32 [32, 16, 3], P('dp'), may hold values from 0 to 15, as said below
- ln1_gain: bfloat16 [1024], P(('dp', 'seq')), may hold values from 0.5 to 1.5
- ln1_shift: bfloat16 [1024], P(('dp', 'seq')), may hold values from -1.5 to 1.5
- query_weight: bfloat16 [1024, 1024], P(('dp', 'seq')), may hold values from -0.1875 to 0.1875
- query_bias: bfloat16 [1024], P(('dp', 'seq')), may hold values from -1.5 to 1.5
- key_weight: bfloat16 [1024, 1024], P(('dp', 'seq')), may hold values from -0.1875 to 0.1875
- value_weight: bfloat16 [1024, 1024], P(('dp', 'seq')), may hold values from -0.1875 to 0.1875
- value_bias: bfloat16 [1024], P(('dp', 'seq')), may hold values from -1.5 to 1.5
- out_weight: bfloat16 [1024, 1024], P(('dp', 'seq')), may hold values from -0.5 to 0.5
- out_bias: bfloat16 [1024], P(('dp', 'seq')), may hold values from -1.5 to 1.5
- ln2_gain: bfloat16 [1024], P(('dp', 'seq')), may hold values from 0.5 to 1.5
- ln2_shift: bfloat16 [1024], P(('dp', 'seq')), may hold values from -1.5 to 1.5
- up_weight: bfloat16 [1024, 4096], P(('dp', 'seq')), may hold values from -0.1875 to 0.1875
- up_bias: bfloat16 [4096], P(('dp', 'seq')), may hold values from -1.5 to 1.5
- down_weight: bfloat16 [4096, 1024], P(('dp', 'seq')), may hold values from -0.125 to 0.125
- down_bias: bfloat16 [1024], P(('dp', 'seq')), may hold values from -1.5 to 1.5
Outputs:
- mixed: bfloat16 [32, 1024, 1024], P('dp', 'seq')
- token_grad: bfloat16 [32, 1024, 1024], P('dp', 'seq')
- grad_ln1_gain: float32 [1024], P(('dp', 'seq'))
- grad_ln1_shift: float32 [1024], P(('dp', 'seq'))
- grad_query_weight: float32 [1024, 1024], P(('dp', 'seq'))
- grad_query_bias: float32 [1024], P(('dp', 'seq'))
- grad_key_weight: float32 [1024, 1024], P(('dp', 'seq'))
- grad_value_weight: float32 [1024, 1024], P(('dp', 'seq'))
- grad_value_bias: float32 [1024], P(('dp', 'seq'))
- grad_out_weight: float32 [1024, 1024], P(('dp', 'seq'))
- grad_out_bias: float32 [1024], P(('dp', 'seq'))
- grad_ln2_gain: float32 [1024], P(('dp', 'seq'))
- grad_ln2_shift: float32 [1024], P(('dp', 'seq'))
- grad_up_weight: float32 [1024, 4096], P(('dp', 'seq'))
- grad_up_bias: float32 [4096], P(('dp', 'seq'))
- grad_down_weight: float32 [4096, 1024], P(('dp', 'seq'))
- grad_down_bias: float32 [1024], P(('dp', 'seq'))
The draws below stay inside these ranges and needn't reach their ends.
Inputs may be any that keep to these rules, and one draw needn't show every extreme that they name: `segments`: each sequence holds four documents numbered 0 to 3 in order; document 0 and 1 end within the first 512 tokens, document 3 starts within the last 512 tokens. `global_blocks`: the first global block lies in the first half of the 16 blocks, the second in the second half. `random_blocks`: random block k of query block j lies in the run of 8 blocks numbered ((j // 8) + 3 * (j % 8) + k) mod (2); it may repeat a window, global or other random block of j, which then counts once.
All inputs are finite; a program needn't handle non-finite values.
Results may differ from the reference program's by a relative error of at most 0.018.
Values may be sent and summed in bfloat16 or wider, within the bound.
No kernel may reach another device: no remote copies, remote signals or barrier semaphores. Data moves between devices by JAX's collectives and lax.ppermute only.
A program may use at most 448 MiB of HBM per device.

```python
import math
import jax
import jax.numpy as jnp
from jax import lax

D = 1024
HEADS = 16
FF = 4096
BLK = 64
BLK_DEV = 8
NB = 16
SEQ_LEN = 1024
SEQS = 32


def draw_segments(key, part):
    key = jax.random.fold_in(key, 11)
    first_key, second_key, third_key = jax.random.split(key, 3)
    local_length = BLK_DEV * BLK
    cut_one = jax.random.randint(first_key, (SEQS, 1), 1, local_length - 1)
    cut_two = cut_one + 1 + jax.random.randint(second_key, (SEQS, 1), 0, local_length - 1 - cut_one)
    cut_three = jax.random.randint(third_key, (SEQS, 1), SEQ_LEN - local_length + 1, SEQ_LEN)
    positions = jnp.arange(SEQ_LEN, dtype=jnp.int32)[None, :]
    numbers = (positions >= cut_one).astype(jnp.int32) + (positions >= cut_two).astype(jnp.int32)
    return numbers + (positions >= cut_three).astype(jnp.int32)


def draw_global_blocks(key, part):
    key = jax.random.fold_in(key, 12)
    first_key, second_key = jax.random.split(key, 2)
    lower = jax.random.randint(first_key, (SEQS, 1), 0, NB // 2)
    upper = jax.random.randint(second_key, (SEQS, 1), NB // 2, NB)
    return jnp.concatenate([lower, upper], axis=1).astype(jnp.int32)


def draw_random_blocks(key, part):
    key = jax.random.fold_in(key, 13)
    query_ids = jnp.arange(NB, dtype=jnp.int32)[:, None]
    member = jnp.arange(3, dtype=jnp.int32)[None, :]
    runs = NB // BLK_DEV
    owner_run = (query_ids // BLK_DEV + 3 * (query_ids % BLK_DEV) + member) % runs
    inside_run = jax.random.randint(key, (SEQS, NB, 3), 0, BLK_DEV)
    return (owner_run[None] * BLK_DEV + inside_run).astype(jnp.int32)


def block_scale(key, shape, shards, least, high):
    def one(position, parts):
        heights = jax.random.uniform(jax.random.fold_in(jax.random.fold_in(key, 6), position), (parts,), jnp.float32, least / len(shards), high / len(shards))
        return jnp.repeat(jnp.exp(heights), shape[position] // parts).reshape((-1,) + (1,) * (len(shape) - position - 1))

    level = one(*shards[0])
    for cut in shards[1:]:
        level = level * one(*cut)
    return level


def gaussian(key, shape, scale, limit, cuts=(), held_as=jnp.bfloat16):
    level = block_scale(key, shape, cuts, -0.22, 0.18) if cuts else 1.0
    entries = jax.random.normal(key, shape, jnp.float32) * scale * level
    return jnp.minimum(jnp.maximum(entries, -limit), limit).astype(held_as)


def setup_inputs(seed: int = 0) -> dict:
    seeds = jax.random.split(jax.random.key(seed), 21)
    tokens = gaussian(seeds[0], (SEQS, SEQ_LEN, D), 1.0, 6.0, ((0, 16), (1, 2)))
    cotangent = gaussian(seeds[1], (SEQS, SEQ_LEN, D), 1.0, 6.0, ((0, 16), (1, 2)))
    segments = draw_segments(jax.random.fold_in(seeds[20], 71), 0)
    global_blocks = draw_global_blocks(jax.random.fold_in(seeds[20], 71), 0)
    random_blocks = draw_random_blocks(jax.random.fold_in(seeds[20], 71), 0)
    ln1_gain = jnp.clip(1.0 + 0.1 * jax.random.normal(seeds[5], (D,), jnp.float32), 0.5, 1.5).astype(jnp.bfloat16)
    ln1_shift = gaussian(seeds[6], (D,), 0.3, 1.5, ((0, 32),))
    query_weight = gaussian(seeds[7], (D, D), D ** -0.5, 0.1875, ((0, 32),))
    query_bias = gaussian(seeds[8], (D,), 0.3, 1.5, ((0, 32),))
    key_weight = gaussian(seeds[9], (D, D), D ** -0.5, 0.1875, ((0, 32),))
    value_weight = gaussian(seeds[10], (D, D), D ** -0.5, 0.1875, ((0, 32),))
    value_bias = gaussian(seeds[11], (D,), 0.3, 1.5, ((0, 32),))
    out_weight = gaussian(seeds[12], (D, D), (D // 8) ** -0.5, 0.5, ((0, 32),))
    out_bias = gaussian(seeds[13], (D,), 0.3, 1.5, ((0, 32),))
    ln2_gain = jnp.clip(1.0 + 0.1 * jax.random.normal(seeds[14], (D,), jnp.float32), 0.5, 1.5).astype(jnp.bfloat16)
    ln2_shift = gaussian(seeds[15], (D,), 0.3, 1.5, ((0, 32),))
    up_weight = gaussian(seeds[16], (D, FF), D ** -0.5, 0.1875, ((0, 32),))
    up_bias = gaussian(seeds[17], (FF,), 0.3, 1.5, ((0, 32),))
    down_weight = gaussian(seeds[18], (FF, D), (FF // 2) ** -0.5, 0.125, ((0, 32),))
    down_bias = gaussian(seeds[19], (D,), 0.3, 1.5, ((0, 32),))
    return {"tokens": tokens, "cotangent": cotangent, "segments": segments, "global_blocks": global_blocks, "random_blocks": random_blocks, "ln1_gain": ln1_gain, "ln1_shift": ln1_shift, "query_weight": query_weight, "query_bias": query_bias, "key_weight": key_weight, "value_weight": value_weight, "value_bias": value_bias, "out_weight": out_weight, "out_bias": out_bias, "ln2_gain": ln2_gain, "ln2_shift": ln2_shift, "up_weight": up_weight, "up_bias": up_bias, "down_weight": down_weight, "down_bias": down_bias}


@jax.custom_vjp
def low(v):
    return lax.optimization_barrier(v.astype(jnp.bfloat16)).astype(jnp.float32)

@jax.custom_vjp
def low_back(v):
    return v

def low_keep(v):
    return (low(v), None)

def low_pass(kept, grad):
    return (grad,)

def back_keep(v):
    return (v, None)

def back_low(kept, grad):
    return (low(grad),)
low.defvjp(low_keep, low_pass)
low_back.defvjp(back_keep, back_low)
EPSILON = 1e-06
HIGHEST = lax.Precision.HIGHEST

def layer_norm(values, gain, shift):
    row_mean = lax.optimization_barrier(jnp.mean(values, -1, keepdims=True))
    centred = values - row_mean
    spread = lax.optimization_barrier(jnp.mean(centred * centred, -1, keepdims=True))
    return centred * lax.rsqrt(spread + EPSILON) * gain + shift

def matmul(left, right):
    return jnp.dot(left, right, precision=HIGHEST)

def block_pattern(globals_pair, randoms):
    numbers = jnp.arange(NB).astype(jnp.int32)
    chosen = (numbers == globals_pair[0]) | (numbers == globals_pair[1])
    nearby = jnp.abs(numbers[:, None] - numbers[None, :]) <= 1
    picked = jnp.any(randoms[:, :, None] == numbers[None, None, :], axis=1)
    return chosen[:, None] | chosen[None, :] | nearby | picked

def attention(queries, keys, values, seg_ids, pattern):
    head_dim = D // HEADS
    scale = head_dim ** (-0.5)
    rows_each = math.gcd(512, SEQ_LEN)
    q_heads = queries.reshape(SEQ_LEN, HEADS, head_dim)
    k_heads = keys.reshape(SEQ_LEN, HEADS, head_dim)
    v_heads = values.reshape(SEQ_LEN, HEADS, head_dim)
    key_block = (jnp.arange(SEQ_LEN) // BLK).astype(jnp.int32)

    def one_block(start):
        q_part = lax.dynamic_slice_in_dim(q_heads, start, rows_each, 0)
        row_ids = (start + jnp.arange(rows_each)).astype(jnp.int32)
        block_ok = jnp.take(pattern, row_ids // BLK, axis=0)
        allowed = jnp.take(block_ok, key_block, axis=1) & (seg_ids[row_ids][:, None] == seg_ids[None, :])
        scores = low_back(jnp.einsum('qhd,khd->hqk', q_part, k_heads, precision=HIGHEST) * scale)
        weights = jnp.where(allowed[None], jnp.exp(scores), 0.0)
        totals = lax.optimization_barrier(jnp.sum(weights, -1))
        summed = low_back(jnp.einsum('hqk,khd->qhd', low(weights), v_heads, precision=HIGHEST))
        return summed / jnp.transpose(totals)[:, :, None]
    starts = jnp.arange(0, SEQ_LEN, rows_each).astype(jnp.int32)
    result = lax.map(jax.checkpoint(one_block), starts)
    return result.reshape(SEQ_LEN, D)

def layer(inputs, seg_ids, globals_pair, randoms, params):
    gain_one, shift_one, w_query, b_query, w_key, w_value, b_value, w_out, b_out, gain_two, shift_two, w_up, b_up, w_down, b_down = params
    normed_one = low(layer_norm(inputs, gain_one, shift_one))
    queries = low(low_back(matmul(normed_one, w_query) + b_query))
    keys = low(low_back(matmul(normed_one, w_key)))
    values = low(low_back(matmul(normed_one, w_value) + b_value))
    context = low(low_back(attention(queries, keys, values, seg_ids, block_pattern(globals_pair, randoms))))
    residual = inputs + low_back(matmul(context, w_out) + b_out)
    normed_two = low(layer_norm(residual, gain_two, shift_two))
    hidden = low_back(matmul(normed_two, w_up) + b_up)
    activated = low(low_back(jax.nn.gelu(hidden, approximate=True)))
    return residual + matmul(activated, w_down) + b_down

def reference(tokens, cotangent, segments, global_blocks, random_blocks, ln1_gain, ln1_shift, query_weight, query_bias, key_weight, value_weight, value_bias, out_weight, out_bias, ln2_gain, ln2_shift, up_weight, up_bias, down_weight, down_bias):
    params = tuple((p.astype(jnp.float32) for p in (ln1_gain, ln1_shift, query_weight, query_bias, key_weight, value_weight, value_bias, out_weight, out_bias, ln2_gain, ln2_shift, up_weight, up_bias, down_weight, down_bias)))

    def one_sequence(running, item):
        inputs, upstream, seg_ids, globals_pair, randoms = item

        def forward(values_in, *weights):
            return layer(values_in, seg_ids, globals_pair, randoms, weights)
        output, pull = jax.vjp(forward, inputs.astype(jnp.float32), *params)
        grads = pull(upstream.astype(jnp.float32))
        updated = tuple((total + grad for total, grad in zip(running, grads[1:])))
        return (updated, (output.astype(jnp.bfloat16), grads[0].astype(jnp.bfloat16)))
    zeros = tuple((jnp.zeros_like(p) for p in params))
    totals, (outputs, input_grads) = lax.scan(one_sequence, zeros, (tokens, cotangent, segments, global_blocks, random_blocks))
    return (outputs, input_grads, totals[0], totals[1], totals[2], totals[3], totals[4], totals[5], totals[6], totals[7], totals[8], totals[9], totals[10], totals[11], totals[12], totals[13], totals[14])
```

```python
from functools import partial
import math

import jax
import jax.numpy as jnp
from jax import lax
from jax.experimental import pallas as pl
from jax.experimental.pallas import tpu as pltpu
from jax.sharding import PartitionSpec as P

HEADS = 16
BLK = 64
EPSILON = 1e-06
MASKED = -1e30
DP, SEQ = "dp", "seq"
BOTH = (DP, SEQ)
BF, F32 = jnp.bfloat16, jnp.float32
NT = (((1,), (1,)), ((), ()))
NN = (((1,), (0,)), ((), ()))
TN = (((0,), (0,)), ((), ()))
VMEM_BYTES = 60 * 2**20
TILE = 256
GROUPS = 2


def dot(left, right, dims=NN):
    return lax.dot_general(left, right, dims, preferred_element_type=F32)


class Grid:
    def __init__(self):
        self.dp = lax.axis_size(DP)
        self.group = lax.axis_size(SEQ)
        self.cube = self.group == 2 and self.dp % 4 == 0
        if self.cube:
            self.nz = self.dp // 4
            place = lax.axis_index(DP)
            self.x = lax.axis_index(SEQ)
            self.z, self.y, self.core = place // 4, place // 2 % 2, place % 2

    def over_x(self, v):
        return lax.ppermute(v, SEQ, [(0, 1), (1, 0)])

    def over_y(self, v):
        return lax.ppermute(v, DP, [(i, i ^ 2) for i in range(self.dp)])

    def over_core(self, v):
        return lax.ppermute(v, DP, [(i, i ^ 1) for i in range(self.dp)])

    def along_z(self, v, k):
        return lax.ppermute(v, DP, [(i, (i + 4 * k) % self.dp) for i in range(self.dp)])

    def device(self, c, y, x, k):
        z = (self.z - k) % self.nz
        return ((z * 2 + (self.y ^ y)) * 2 + (self.core ^ c)) * 2 + (self.x ^ x)


class Weight:
    def __init__(self, shape):
        self.shape, self.arrays, self.copies, self.rows_at = shape, [], [], []

    def add(self, array, index, rows, row, source=0, width=None, target=0):
        for i, known in enumerate(self.arrays):
            if known is array:
                break
        else:
            i = len(self.arrays)
            self.arrays.append(array)
        self.copies.append((i, index, rows, source, width or array.shape[-1], target))
        self.rows_at.append(row)


def whole_weight(array):
    weight = Weight(array.shape)
    weight.add(array, None, array.shape[0], 0)
    return weight


def weight_of(parts, width):
    pieces = parts[0][0]
    weight = Weight((len(pieces) * pieces[0][0].shape[1], width))
    for pieces, source, columns, target in parts:
        for array, index, device in pieces:
            rows = array.shape[1]
            weight.add(array, index, rows, device * rows, source, columns, target)
    return weight


def gather_pieces(grid, shard, z_first):
    pieces = []
    if not grid.cube:
        every = lax.all_gather(shard, BOTH, axis=0)
        return [(every, i, i) for i in range(every.shape[0])]
    if z_first:
        own = jnp.stack([shard] + [grid.along_z(shard, k) for k in range(1, grid.nz)])
        half = {(0, 0): own, (0, 1): grid.over_x(own)}
        for x in range(2):
            half[1, x] = grid.over_y(half[0, x])
        for (y, x), piece in half.items():
            for c, array in enumerate((piece, grid.over_core(piece))):
                for k in range(grid.nz):
                    pieces.append((array, k, grid.device(c, y, x, k)))
    else:
        pair = jnp.stack([shard, grid.over_x(shard)])
        four = jnp.concatenate([pair, grid.over_y(pair)])
        for k in range(grid.nz):
            piece = four if k == 0 else grid.along_z(four, k)
            for c, array in enumerate((piece, grid.over_core(piece))):
                for j in range(4):
                    pieces.append((array, j, grid.device(c, j // 2, j % 2, k)))
    return pieces


def run(kernel, weights, ins, outs, steps, flops, scratch=(), scalars=()):
    rows_at = [row for w in weights for row in w.rows_at] + list(scalars)
    rows_at = jnp.stack([jnp.asarray(row, jnp.int32) for row in rows_at] or [jnp.int32(0)])
    n_copies = sum(len(w.copies) for w in weights)
    n_pieces = [len(w.arrays) for w in weights]

    def body(at, *refs):
        refs = list(refs)

        def take(count):
            taken, refs[:count] = refs[:count], []
            return taken

        piece_refs = [take(count) for count in n_pieces]
        in_refs, out_refs = take(len(ins)), take(len(outs))
        held = take(len(weights))
        sems = take(1)[0] if n_copies else None

        def copies():
            n = 0
            for weight, sources, target_ref in zip(weights, piece_refs, held):
                for i, index, rows, source, width, target in weight.copies:
                    ref = sources[i] if index is None else sources[i].at[index]
                    row = pl.multiple_of(at[n], rows)
                    yield pltpu.make_async_copy(
                        ref.at[:, pl.ds(source, width)],
                        target_ref.at[pl.ds(row, rows), pl.ds(target, width)],
                        sems.at[n],
                    )
                    n += 1

        if n_copies:

            @pl.when(pl.program_id(0) == 0)
            def _():
                for copy in copies():
                    copy.start()
                for copy in copies():
                    copy.wait()

        values = [at[n_copies + i] for i in range(len(scalars))]
        kernel(values, in_refs, out_refs, held, refs)

    anywhere = pl.BlockSpec(memory_space=pl.ANY)

    def spec(block, index):
        return pl.BlockSpec(block, lambda i, at: index(i))

    moved = sum(math.prod(w.shape) * 2 for w in weights)
    moved += sum(a.size * a.dtype.itemsize for a, _, _ in ins)
    moved += sum(math.prod(s) * jnp.dtype(d).itemsize for s, d, _, _ in outs)
    semaphores = [pltpu.SemaphoreType.DMA((n_copies,))] if n_copies else []
    return pl.pallas_call(
        body,
        grid_spec=pltpu.PrefetchScalarGridSpec(
            num_scalar_prefetch=1,
            grid=(steps,),
            in_specs=[anywhere] * sum(n_pieces) + [spec(block, index) for _, block, index in ins],
            out_specs=[spec(block, index) for _, _, block, index in outs],
            scratch_shapes=[pltpu.VMEM(w.shape, BF) for w in weights] + semaphores + list(scratch),
        ),
        out_shape=[jax.ShapeDtypeStruct(shape, dtype) for shape, dtype, _, _ in outs],
        compiler_params=pltpu.CompilerParams(vmem_limit_bytes=VMEM_BYTES),
        cost_estimate=pl.CostEstimate(flops=int(flops), bytes_accessed=moved, transcendentals=0),
    )(rows_at, *[a for w in weights for a in w.arrays], *[a for a, _, _ in ins])


def pick(array, index, axis):
    return lax.dynamic_index_in_dim(array, index, axis, keepdims=False)


def halve(kept, got, mine, axis, move):
    sent = (pick(kept, 1 - mine, axis).astype(F32) + pick(got, 1 - mine, axis).astype(F32)).astype(kept.dtype)
    own = (pick(kept, mine, axis).astype(F32) + pick(got, mine, axis).astype(F32)).astype(kept.dtype)
    return own, move(sent)


def scatter_sum(grid, kept, sent, z_first):
    got = grid.over_core(sent)
    if z_first:
        parts = []
        for k in range(grid.nz):
            z = (grid.z + k) % grid.nz
            parts.append((pick(kept, z, 0).astype(F32) + pick(got, z, 0).astype(F32)).astype(kept.dtype))
        total = parts[0].astype(F32)
        for k in range(1, grid.nz):
            total = total + grid.along_z(parts[k], k).astype(F32)
        total = total.astype(kept.dtype)
        got = grid.over_y(pick(total, 1 - grid.y, 0))
        total = (pick(total, grid.y, 0).astype(F32) + got.astype(F32)).astype(kept.dtype)
        got = grid.over_x(pick(total, 1 - grid.x, 0))
        return pick(total, grid.x, 0).astype(F32) + got.astype(F32)
    own, got = halve(kept, got, grid.y, 1, grid.over_y)
    own, got = halve(own, got, grid.x, 1, grid.over_x)
    total = pick(own, grid.z, 0).astype(F32) + pick(got, grid.z, 0).astype(F32)
    for k in range(1, grid.nz):
        z = (grid.z + k) % grid.nz
        part = (pick(own, z, 0).astype(F32) + pick(got, z, 0).astype(F32)).astype(kept.dtype)
        total = total + grid.along_z(part, k).astype(F32)
    return total


def to_whole(grid, part):
    group, count = grid.group, part.shape[0]
    if group == 1:
        return part
    place = lax.axis_index(SEQ)
    if group == 2 and count == 2:
        kept, got = pick(part, place, 0), grid.over_x(pick(part, 1 - place, 0))
        first = jnp.where(place == 0, kept, got)
        second = jnp.where(place == 0, got, kept)
        return jnp.concatenate([first, second])[None]
    if count % group == 0:
        return lax.all_to_all(part, SEQ, split_axis=0, concat_axis=1, tiled=True)
    every = lax.all_gather(part, SEQ, axis=1, tiled=True)
    return pick(every, place % count, 0)[None]


def from_whole(grid, whole, count):
    group = grid.group
    if group == 1:
        return whole
    place = lax.axis_index(SEQ)
    if group == 2 and count == 2:
        halves = whole.reshape(2, -1, whole.shape[-1])
        kept, got = pick(halves, place, 0), grid.over_x(pick(halves, 1 - place, 0))
        first = jnp.where(place == 0, kept, got)
        second = jnp.where(place == 0, got, kept)
        return jnp.stack([first, second])
    if count % group == 0:
        return lax.all_to_all(whole, SEQ, split_axis=1, concat_axis=0, tiled=True)
    every = lax.all_gather(whole[0], SEQ, axis=0)[:count]
    rows = whole.shape[1] // group
    return lax.dynamic_slice_in_dim(every, place * rows, rows, 1)


def attention_forward_kernel(q_ref, k_ref, v_ref, mask_ref, out_ref, total_ref, *, head, chunk):
    factor = head**-0.5 * math.log2(math.e)
    rows = q_ref.shape[1]
    for h in range(q_ref.shape[2] // head):
        lanes = slice(h * head, (h + 1) * head)
        keys, values = k_ref[0, :, lanes], v_ref[0, :, lanes]
        for start in range(0, rows, chunk):
            part = slice(start, start + chunk)
            scores = dot(keys, q_ref[0, part, lanes], NT)
            weights = jnp.exp2(scores * factor + mask_ref[0, :, part])
            total = jnp.sum(weights, axis=0, keepdims=True)
            summed = dot(values, weights.astype(BF), TN)
            total_ref[0, 0, h : h + 1, part] = total
            out_ref[0, part, lanes] = (summed / total).T.astype(BF)


def attention_backward_kernel(
    q_ref, k_ref, v_ref, mask_ref, grad_ref, ctx_ref, total_ref, out_ref, dk_sum, dv_sum, *, head, chunk
):
    scale = head**-0.5
    factor = scale * math.log2(math.e)
    rows = q_ref.shape[1]
    for h in range(q_ref.shape[2] // head):
        lanes = slice(h * head, (h + 1) * head)
        keys, values = k_ref[0, :, lanes], v_ref[0, :, lanes]
        keys_t = keys.T
        for start in range(0, rows, chunk):
            part = slice(start, start + chunk)
            queries = q_ref[0, part, lanes]
            scores = dot(keys, queries, NT)
            weights = jnp.exp2(scores * factor + mask_ref[0, :, part])
            inverse = 1.0 / total_ref[0, 0, h : h + 1, part]
            grad = grad_ref[0, part, lanes].astype(F32)
            product = (grad * ctx_ref[0, part, lanes].astype(F32)).T
            grad_total = -jnp.sum(product, axis=0, keepdims=True) * inverse
            grad_summed = (grad.T * inverse).astype(BF)
            grad_probs = dot(values, grad_summed)
            grad_scores = (weights * (grad_probs + grad_total)).astype(BF)
            dv_part = dot(weights.astype(BF), grad_summed, NT)
            dk_part = dot(grad_scores, queries)
            if start == 0:
                dv_sum[...] = dv_part
                dk_sum[...] = dk_part
            else:
                dv_sum[...] += dv_part
                dk_sum[...] += dk_part
            out_ref[0, 0, part, lanes] = (dot(keys_t, grad_scores).T * scale).astype(BF)
        out_ref[1, 0, :, lanes] = (dk_sum[...] * scale).astype(BF)
        out_ref[2, 0, :, lanes] = dv_sum[...].astype(BF)


def attention_specs(length, width, group):
    head = width // HEADS
    lanes = max(128, head)
    steps = width // lanes // GROUPS

    def columns(which):
        return pl.BlockSpec((1, length, lanes), lambda b, p: (b, 0, (which * GROUPS + group) * steps + p))

    own = pl.BlockSpec((1, length, lanes), lambda b, p: (b, 0, p))
    mask = pl.BlockSpec((1, length, length), lambda b, p: (b, 0, 0))
    totals = pl.BlockSpec((1, 1, lanes // head, length), lambda b, p: (b, p, 0, 0))
    return head, lanes, steps, columns, own, mask, totals


def attention_forward(qkv, mask, group):
    count, length, width = qkv.shape
    width = width // 3
    head, lanes, steps, columns, own, mask_spec, totals = attention_specs(length, width, group)
    return pl.pallas_call(
        partial(attention_forward_kernel, head=head, chunk=512),
        grid=(count, steps),
        in_specs=[columns(0), columns(1), columns(2), mask_spec],
        out_specs=[own, totals],
        out_shape=[
            jax.ShapeDtypeStruct((count, length, width // GROUPS), BF),
            jax.ShapeDtypeStruct((count, steps, lanes // head, length), F32),
        ],
        compiler_params=pltpu.CompilerParams(vmem_limit_bytes=VMEM_BYTES),
        cost_estimate=pl.CostEstimate(
            flops=12 * count * length * length * width // GROUPS, bytes_accessed=12 * 2**20, transcendentals=0
        ),
    )(qkv, qkv, qkv, mask)


def attention_backward(qkv, mask, grad, context, totals_in, group):
    count, length, width = grad.shape
    head, lanes, steps, columns, own, mask_spec, totals = attention_specs(length, width, group)
    grads = pl.BlockSpec((3, 1, length, lanes), lambda b, p: (0, b, 0, p))
    return pl.pallas_call(
        partial(attention_backward_kernel, head=head, chunk=256),
        grid=(count, steps),
        in_specs=[columns(0), columns(1), columns(2), mask_spec, columns(0), own, totals],
        out_specs=grads,
        out_shape=jax.ShapeDtypeStruct((3, count, length, width // GROUPS), BF),
        scratch_shapes=[pltpu.VMEM((length, head), F32)] * 2,
        compiler_params=pltpu.CompilerParams(vmem_limit_bytes=VMEM_BYTES),
        cost_estimate=pl.CostEstimate(
            flops=26 * count * length * length * width // GROUPS, bytes_accessed=20 * 2**20, transcendentals=0
        ),
    )(qkv, qkv, qkv, mask, grad, context, totals_in)


def attention_mask(segments, globals_pair, randoms):
    count, blocks = randoms.shape[:2]
    length = segments.shape[1]
    numbers = jnp.arange(blocks, dtype=jnp.int32)
    chosen = jnp.any(globals_pair[:, :, None] == numbers, axis=1)
    nearby = jnp.abs(numbers[:, None] - numbers[None, :]) <= 1
    picked = jnp.any(randoms[:, :, :, None] == numbers, axis=2)
    seen = chosen[:, :, None] | chosen[:, None, :] | nearby[None] | picked
    seen = jnp.swapaxes(seen, 1, 2)[:, :, None, :, None]
    seen = jnp.broadcast_to(seen, (count, blocks, BLK, blocks, BLK)).reshape(count, length, length)
    same = segments[:, :, None] == segments[:, None, :]
    return jnp.where(seen & same, 0.0, MASKED).astype(F32)


def normalise(values):
    centred = values - jnp.mean(values, -1, keepdims=True)
    inverse = lax.rsqrt(jnp.mean(centred * centred, -1, keepdims=True) + EPSILON)
    return centred * inverse, inverse


def normalise_back(grad, values, gain):
    unit, inverse = normalise(values)
    inner = grad * gain
    grad_in = inverse * (
        inner - jnp.mean(inner, -1, keepdims=True) - unit * jnp.mean(inner * unit, -1, keepdims=True)
    )
    return grad_in, jnp.sum(grad * unit, 0, keepdims=True), jnp.sum(grad, 0, keepdims=True)


def accumulate(ref, rows):
    first = pl.program_id(0) == 0
    for j, row in enumerate(rows):

        @pl.when(first)
        def _():
            ref[j : j + 1] = row

        @pl.when(jnp.logical_not(first))
        def _():
            ref[j : j + 1] += row


def row_block(i):
    return (i, 0)


def fixed_block(i):
    return (0, 0)


def column_block(i):
    return (0, i)


def project_in(x, w_qkv, extra):
    rows, width = x.shape

    def kernel(_, ins, outs, weights, scratch):
        qkv, turned, params = outs
        w, small = weights

        @pl.when(pl.program_id(0) == 0)
        def _():
            params[...] = small[...].astype(F32).T[:16]

        unit, _ = normalise(ins[0][...].astype(F32))
        normed = (unit * params[0:1] + params[1:2]).astype(BF)
        turned[...] = normed.T
        for part, bias in enumerate((params[2:3], None, params[3:4])):
            columns = slice(part * width, (part + 1) * width)
            value = dot(normed, w[:, columns])
            qkv[:, columns] = (value if bias is None else value + bias).astype(BF)

    return run(
        kernel,
        [w_qkv, extra],
        [(x, (TILE, width), row_block)],
        [
            ((rows, 3 * width), BF, (TILE, 3 * width), row_block),
            ((width, rows), BF, (width, TILE), column_block),
            ((16, width), F32, (16, width), fixed_block),
        ],
        rows // TILE,
        6 * rows * width * width,
    )


def project_out(contexts, x, params, w_o):
    rows, width = x.shape

    def kernel(_, ins, outs, weights, scratch):
        x_ref, params = ins[:2]
        residual, normed, turned, context_turned = outs
        parts = [ref[...] for ref in ins[2:]]
        context = jnp.concatenate(parts, axis=1)
        context_turned[...] = context.T
        value = x_ref[...].astype(F32) + dot(context, weights[0][...]) + params[4:5]
        residual[...] = value
        unit, _ = normalise(value)
        low = (unit * params[5:6] + params[6:7]).astype(BF)
        normed[...] = low
        turned[...] = low.T

    return run(
        kernel,
        [w_o],
        [(x, (TILE, width), row_block), (params, (16, width), fixed_block)]
        + [(c, (TILE, c.shape[1]), row_block) for c in contexts],
        [
            ((rows, width), F32, (TILE, width), row_block),
            ((rows, width), BF, (TILE, width), row_block),
            ((width, rows), BF, (width, TILE), column_block),
            ((width, rows), BF, (width, TILE), column_block),
        ],
        rows // TILE,
        2 * rows * width * width,
    )


def feed_up(normed, w_up, bias):
    rows, width = normed.shape
    wide = w_up.shape[1]
    outer = math.sqrt(2 / math.pi)
    cubic = 0.044715

    def kernel(_, ins, outs, weights, scratch):
        value, slope = outs
        for start in range(0, wide, width):
            columns = slice(start, start + width)
            u = dot(ins[0][...], weights[0][:, columns]) + ins[1][:, columns]
            square = u * u
            half = 0.5 + 0.5 * jnp.tanh(u * (outer + outer * cubic * square))
            gelu = u * half
            value[:, columns] = gelu.astype(BF)
            rest = gelu * (1.0 - half) * (2 * outer + 6 * outer * cubic * square)
            slope[:, columns] = (half + rest).astype(BF)

    return run(
        kernel,
        [w_up],
        [(normed, (TILE, width), row_block), (bias, (1, wide), fixed_block)],
        [((rows, wide), BF, (TILE, wide), row_block)] * 2,
        rows // TILE,
        2 * rows * width * wide,
    )


def feed_down(activated, slope, residual, upstream, params, w_down):
    rows, wide = activated.shape
    width = residual.shape[1]

    def kernel(_, ins, outs, weights, scratch):
        act, slope, residual, upstream, params = ins
        mixed, grad_hidden, sum_up, sum_down = outs
        w = weights[0]
        value = residual[...] + dot(act[...], w[...]) + params[7:8]
        mixed[...] = value.astype(BF)
        dy = upstream[...]
        sums = []
        for start in range(0, wide, width):
            columns = slice(start, start + width)
            grad = dot(dy, w[columns, :], NT).astype(BF).astype(F32)
            low = (grad * slope[:, columns].astype(F32)).astype(BF)
            grad_hidden[:, columns] = low
            sums.append(jnp.sum(low.astype(F32), 0, keepdims=True))
        accumulate(sum_up, [jnp.concatenate(sums, axis=1)])
        accumulate(sum_down, [jnp.sum(dy.astype(F32), 0, keepdims=True)])

    return run(
        kernel,
        [w_down],
        [
            (activated, (TILE, wide), row_block),
            (slope, (TILE, wide), row_block),
            (residual, (TILE, width), row_block),
            (upstream, (TILE, width), row_block),
            (params, (16, width), fixed_block),
        ],
        [
            ((rows, width), BF, (TILE, width), row_block),
            ((rows, wide), BF, (TILE, wide), row_block),
            ((8, wide), F32, (8, wide), fixed_block),
            ((8, width), F32, (8, width), fixed_block),
        ],
        rows // TILE,
        4 * rows * width * wide,
    )


def feed_back(grad_hidden, residual, upstream, params, w_up, w_o):
    rows, width = residual.shape
    wide = grad_hidden.shape[1]

    def kernel(_, ins, outs, weights, scratch):
        du, residual, upstream, params = ins
        grad_residual, grad_att, grad_context, sums = outs
        grad = dot(du[...], weights[0][...], NT)
        part, gain, shift = normalise_back(grad, residual[...], params[5:6])
        total = upstream[...].astype(F32) + part
        grad_residual[...] = total
        low = total.astype(BF)
        grad_att[...] = low
        grad_context[...] = dot(low, weights[1][...], NT).astype(BF)
        accumulate(sums, [jnp.sum(low.astype(F32), 0, keepdims=True), gain, shift])

    return run(
        kernel,
        [w_up, w_o],
        [
            (grad_hidden, (TILE, wide), row_block),
            (residual, (TILE, width), row_block),
            (upstream, (TILE, width), row_block),
            (params, (16, width), fixed_block),
        ],
        [
            ((rows, width), F32, (TILE, width), row_block),
            ((rows, width), BF, (TILE, width), row_block),
            ((rows, width), BF, (TILE, width), row_block),
            ((8, width), F32, (8, width), fixed_block),
        ],
        rows // TILE,
        2 * rows * width * (wide + width),
    )


def project_back(grads, grad_residual, x, params, w_qkv):
    rows, width = x.shape
    each = width // GROUPS

    def kernel(_, ins, outs, weights, scratch):
        grad_residual, x_ref, params = ins[:3]
        grad_in, sums = outs
        w = weights[0]
        grad = None
        biases = []
        for part in range(3):
            cut = [ref[part] for ref in ins[3:]]
            low = jnp.concatenate(cut, axis=1)
            if part != 1:
                biases.append(jnp.sum(low.astype(F32), 0, keepdims=True))
            value = dot(low, w[:, part * width : (part + 1) * width], NT)
            grad = value if grad is None else grad + value
        part, gain, shift = normalise_back(grad, x_ref[...].astype(F32), params[0:1])
        grad_in[...] = (grad_residual[...] + part).astype(BF)
        accumulate(sums, [gain, shift] + biases)

    return run(
        kernel,
        [w_qkv],
        [
            (grad_residual, (TILE, width), row_block),
            (x, (TILE, width), row_block),
            (params, (16, width), fixed_block),
        ]
        + [(g, (3, TILE, each), lambda i: (0, i, 0)) for g in grads],
        [
            ((rows, width), BF, (TILE, width), row_block),
            ((8, width), F32, (8, width), fixed_block),
        ],
        rows // TILE,
        6 * rows * width * width,
    )


def weight_grad(grid, turned, right):
    features, rows = turned.shape
    parts, _, columns = right.shape
    tile = min(512, columns)
    per = columns // tile
    pair = features // grid.nz // 4

    def kernel(scalars, ins, outs, weights, scratch):
        kept, sent = outs
        first = scalars[0] == 0
        value = dot(ins[0][...], ins[1][0]).astype(BF)
        for j in range(grid.nz * 2):
            low = value[2 * j * pair : (2 * j + 1) * pair]
            high = value[(2 * j + 1) * pair : (2 * j + 2) * pair]
            kept[j * pair : (j + 1) * pair] = jnp.where(first, low, high)
            sent[j * pair : (j + 1) * pair] = jnp.where(first, high, low)

    kept, sent = run(
        kernel,
        [],
        [
            (turned, (features, rows), fixed_block),
            (right, (1, rows, tile), lambda i: (i // per, 0, i % per)),
        ],
        [((features // 2, parts * columns), BF, (features // 2, tile), column_block)] * 2,
        parts * per,
        2 * rows * features * parts * columns,
        scalars=[grid.core],
    )
    shape = (grid.nz, 2, 2, pair // 2, parts * columns)
    return kept.reshape(shape), sent.reshape(shape)


def weight_grad_turned(turned, right, devices):
    features, rows = turned.shape
    columns = right.shape[1]
    each = columns // devices
    tile = min(512, columns)

    def kernel(_, ins, outs, weights, scratch):
        value = dot(ins[0][...], ins[1][...]).astype(BF)
        for j in range(tile // each):
            outs[0][j] = value[:, j * each : (j + 1) * each]

    return run(
        kernel,
        [],
        [(turned, (features, rows), fixed_block), (right, (rows, tile), column_block)],
        [((devices, features, each), BF, (tile // each, features, each), lambda i: (i, 0, 0))],
        columns // tile,
        2 * rows * features * columns,
    )[0]


def shards(tokens, cotangent, segments, global_blocks, random_blocks, *params):
    grid = Grid()
    gain1, shift1, w_q, b_q, w_k, w_v, b_v, w_o, b_o, gain2, shift2, w_up, b_up, w_down, b_down = params
    count = tokens.shape[0]
    width = tokens.shape[-1]
    each = w_v.shape[0]
    devices = grid.dp * grid.group
    replicas = max(1, grid.group // count)

    inputs = to_whole(grid, tokens)
    n, length = inputs.shape[:2]
    rows = n * length
    inputs = inputs.reshape(rows, width)
    vectors = [gain1, shift1, b_q, b_v, b_o, gain2, shift2, b_down]
    extra = jnp.concatenate([jnp.stack(vectors, axis=1), b_up.reshape(each, -1)], axis=1)
    extra = jnp.pad(extra, ((0, 0), (0, 128 - extra.shape[1])))
    pieces_qk = gather_pieces(grid, jnp.concatenate([w_q, w_k], axis=1), True)
    pieces_v = gather_pieces(grid, jnp.concatenate([w_v, extra], axis=1), False)
    w_qkv = weight_of([(pieces_qk, 0, 2 * width, 0), (pieces_v, 0, width, 2 * width)], 3 * width)
    extra = weight_of([(pieces_v, width, 128, 0)], 128)
    w_o = weight_of([(gather_pieces(grid, w_o, False), 0, width, 0)], width)
    w_up = whole_weight(lax.all_gather(w_up, BOTH, axis=0, tiled=True))
    w_down = whole_weight(lax.all_gather(w_down, BOTH, axis=0, tiled=True))
    upstream = to_whole(grid, cotangent).reshape(rows, width)
    upstream_turned = upstream.T

    if grid.group > 1:
        place = lax.axis_index(SEQ)
        first = place * n if count % grid.group == 0 else place % count
        segments, global_blocks, random_blocks = (
            lax.dynamic_slice_in_dim(a, first, n, 0) for a in (segments, global_blocks, random_blocks)
        )
    mask = attention_mask(segments, global_blocks, random_blocks)

    qkv, normed1_turned, params = project_in(inputs, w_qkv, extra)
    qkv = qkv.reshape(n, length, 3 * width)
    attended = [attention_forward(qkv, mask, g) for g in range(GROUPS)]
    contexts = [a[0].reshape(rows, -1) for a in attended]
    residual, normed2, normed2_turned, context_turned = project_out(contexts, inputs, params, w_o)
    bias_up = params[8:12].T.reshape(1, -1)
    activated, slope = feed_up(normed2, w_up, bias_up)

    grad_w_down = weight_grad_turned(upstream_turned, activated, devices)
    mixed, grad_hidden, sum_up, sum_down = feed_down(activated, slope, residual, upstream, params, w_down)
    mixed = from_whole(grid, mixed.reshape(n, length, width), count)
    terms_up = weight_grad_of(grid, normed2_turned, grad_hidden[None])
    grad_residual, grad_att, grad_context, sums2 = feed_back(
        grad_hidden, residual, upstream, params, w_up, w_o
    )
    terms_o = weight_grad_of(grid, context_turned, grad_att[None])
    grad_context = grad_context.reshape(n, length, width)
    grads, terms_qkv = [], []
    for g in range(GROUPS):
        grad = attention_backward(qkv, mask, grad_context, *attended[g], g)
        grads.append(grad.reshape(3, rows, -1))
        terms_qkv.append(weight_grad_of(grid, normed1_turned, grads[g]))
    grad_inputs, sums1 = project_back(grads, grad_residual, inputs, params, w_qkv)
    grad_inputs = from_whole(grid, grad_inputs.reshape(n, length, width), count)

    share = 1.0 / replicas
    grad_w_down = lax.psum_scatter(grad_w_down * BF(share), BOTH, scatter_dimension=0, tiled=True)
    grad_w_down = grad_w_down[0].T.astype(F32)
    grad_w_up = sum_up_devices(grid, terms_up, False) * share
    grad_w_o = sum_up_devices(grid, terms_o, True) * share
    ended = [sum_up_devices(grid, t, False) * share for t in terms_qkv]
    cut = width // GROUPS
    grad_w_q, grad_w_k, grad_w_v = (
        jnp.concatenate([e[:, j * cut : (j + 1) * cut] for e in ended], axis=1) for j in range(3)
    )
    vectors = jnp.concatenate([sums1[:4], sums2[:3], sum_down[:1]])
    vectors = vectors.reshape(8, devices, each).transpose(1, 0, 2).reshape(devices, -1)
    vectors = jnp.concatenate([vectors, sum_up[:1].reshape(devices, -1)], axis=1)
    if grid.cube:
        vectors = vectors.reshape(grid.nz, 2, 2, 2, -1, 128)
        vectors = scatter_sum(grid, pick(vectors, grid.core, 2), pick(vectors, 1 - grid.core, 2), False)
    else:
        vectors = lax.psum_scatter(vectors, BOTH, scatter_dimension=0, tiled=True) * share
    vectors = vectors.reshape(-1)
    grad_b_up = vectors[8 * each :]
    grad_gain1, grad_shift1, grad_b_q, grad_b_v, grad_b_o, grad_gain2, grad_shift2, grad_b_down = (
        vectors[j * each : (j + 1) * each] for j in range(8)
    )
    return (
        mixed, grad_inputs, grad_gain1, grad_shift1, grad_w_q, grad_b_q, grad_w_k, grad_w_v, grad_b_v,
        grad_w_o, grad_b_o, grad_gain2, grad_shift2, grad_w_up, grad_b_up, grad_w_down, grad_b_down,
    )


def weight_grad_of(grid, turned, right):
    if grid.cube:
        return weight_grad(grid, turned, right)
    return [dot(turned, part) for part in right]


def sum_up_devices(grid, terms, z_first):
    if grid.cube:
        return scatter_sum(grid, *terms, z_first)
    whole = jnp.concatenate(terms, axis=1)
    return lax.psum_scatter(whole, BOTH, scatter_dimension=0, tiled=True)


def solution(mesh):
    rows = P(DP, SEQ, None)
    vector, matrix = P(BOTH), P(BOTH, None)
    params = (
        vector, vector, matrix, vector, matrix, matrix, vector, matrix, vector, vector, vector, matrix,
        vector, matrix, vector,
    )
    in_specs = (rows, rows, P(DP, None), P(DP, None), P(DP, None, None)) + params
    out_specs = (rows, rows) + params
    return jax.shard_map(shards, mesh=mesh, in_specs=in_specs, out_specs=out_specs, check_vma=False)
```

```python
from functools import partial
import math

import jax
import jax.numpy as jnp
from jax import lax
from jax.experimental import pallas as pl
from jax.experimental.pallas import tpu as pltpu
from jax.sharding import PartitionSpec as P

HEADS = 16
BLK = 64
EPSILON = 1e-06
MASKED = -1e30
DP, SEQ = "dp", "seq"
BOTH = (DP, SEQ)
BF, F32 = jnp.bfloat16, jnp.float32
NT = (((1,), (1,)), ((), ()))
NN = (((1,), (0,)), ((), ()))
TN = (((0,), (0,)), ((), ()))
VMEM_BYTES = 60 * 2**20
TILE = 256
GROUPS = 2
LONG, SHORT = 5.0, 0.05
WG, SUM = "weight_grad_", "sum_"


def cost(flops, nbytes=0):
    return pl.CostEstimate(flops=int(flops), bytes_accessed=int(nbytes), transcendentals=0)


def dot(left, right, dims=NN):
    return lax.dot_general(left, right, dims, preferred_element_type=F32)


class Grid:
    def __init__(self):
        self.dp = lax.axis_size(DP)
        self.group = lax.axis_size(SEQ)
        self.cube = self.group == 2 and self.dp % 4 == 0
        if self.cube:
            self.nz = self.dp // 4
            place = lax.axis_index(DP)
            self.x = lax.axis_index(SEQ)
            self.z, self.y, self.core = place // 4, place // 2 % 2, place % 2

    def over_x(self, v):
        return lax.ppermute(v, SEQ, [(0, 1), (1, 0)])

    def over_y(self, v):
        return lax.ppermute(v, DP, [(i, i ^ 2) for i in range(self.dp)])

    def over_xy(self, v):
        pairs = [(2 * i + x, 2 * (i ^ 2) + 1 - x) for i in range(self.dp) for x in range(2)]
        return lax.ppermute(v, BOTH, pairs)

    def over_core(self, v):
        return lax.ppermute(v, DP, [(i, i ^ 1) for i in range(self.dp)])

    def along_z(self, v, k):
        return lax.ppermute(v, DP, [(i, (i + 4 * k) % self.dp) for i in range(self.dp)])

    def device(self, c, y, x, k):
        z = (self.z - k) % self.nz
        return ((z * 2 + (self.y ^ y)) * 2 + (self.core ^ c)) * 2 + (self.x ^ x)


class Weight:
    def __init__(self, shape):
        self.shape, self.arrays, self.copies, self.rows_at = shape, [], [], []

    def add(self, array, index, rows, row, source=0, width=None, target=0):
        for i, known in enumerate(self.arrays):
            if known is array:
                break
        else:
            i = len(self.arrays)
            self.arrays.append(array)
        self.copies.append((i, index, rows, source, width or array.shape[-1], target))
        self.rows_at.append(row)


def whole_weight(array):
    weight = Weight(array.shape)
    weight.add(array, None, array.shape[0], 0)
    return weight


def columns_of(*parts):
    pieces = parts[0][0]
    weight = Weight((len(pieces) * pieces[0][0].shape[1], sum(width for _, _, width in parts)))
    target = 0
    for pieces, start, width in parts:
        for array, index, device in pieces:
            rows = array.shape[1]
            weight.add(array, index, rows, device * rows, start, width, target)
        target += width
    return weight


def gather(shard):
    every = lax.all_gather(shard, BOTH, axis=0)
    return [(every, i, i) for i in range(every.shape[0])]


class Gather:
    def __init__(self, grid, shard):
        self.grid = grid
        if not grid.cube:
            self.all = gather(shard)
            return
        shard = shard[None]
        self.got = [shard] + [grid.along_z(shard, k) for k in range(1, grid.nz)]

    def near(self, clock, wait):
        if not self.grid.cube:
            return wait
        own = jnp.concatenate(self.got)
        own, wait = clock(own, wait)
        self.got = [own, self.grid.over_xy(own), self.grid.over_x(own), self.grid.over_y(own)]
        return wait

    def pieces(self, clock):
        grid = self.grid
        if not grid.cube:
            return self.all
        self.got = clock(*self.got)
        pieces = []
        for (y, x), piece in zip(((0, 0), (1, 1), (0, 1), (1, 0)), self.got):
            for c, array in enumerate((piece, grid.over_core(piece))):
                pieces += [(array, k, grid.device(c, y, x, k)) for k in range(grid.nz)]
        return pieces


class Clock:
    def __init__(self):
        self.token = None

    def __call__(self, *values):
        if self.token is None:
            self.token = jnp.zeros((8, 128), F32)
        *values, self.token = lax.optimization_barrier((*values, self.token))
        return values[0] if len(values) == 1 else values


def run(kernel, weights, ins, outs, steps, flops, scratch=(), scalars=(), name=None, share=SHORT):
    rows_at = [row for w in weights for row in w.rows_at] + list(scalars)
    rows_at = jnp.stack([jnp.asarray(row, jnp.int32) for row in rows_at] or [jnp.int32(0)])
    n_copies = sum(len(w.copies) for w in weights)
    n_pieces = [len(w.arrays) for w in weights]

    def body(at, *refs):
        refs = list(refs)

        def take(count):
            taken, refs[:count] = refs[:count], []
            return taken

        piece_refs = [take(count) for count in n_pieces]
        in_refs, out_refs = take(len(ins)), take(len(outs))
        held = take(len(weights))
        sems = take(1)[0] if n_copies else None

        def copies():
            n = 0
            for weight, sources, target_ref in zip(weights, piece_refs, held):
                for i, index, rows, source, width, target in weight.copies:
                    ref = sources[i] if index is None else sources[i].at[index]
                    row = pl.multiple_of(at[n], rows)
                    yield pltpu.make_async_copy(
                        ref.at[:, pl.ds(source, width)],
                        target_ref.at[pl.ds(row, rows), pl.ds(target, width)],
                        sems.at[n],
                    )
                    n += 1

        if n_copies:

            @pl.when(pl.program_id(0) == 0)
            def _():
                for copy in copies():
                    copy.start()
                for copy in copies():
                    copy.wait()

        values = [at[n_copies + i] for i in range(len(scalars))]
        kernel(values, in_refs, out_refs, held, refs)

    anywhere = pl.BlockSpec(memory_space=pl.ANY)

    def spec(block, index):
        if index is shifted_row_block:
            return pl.BlockSpec(block, lambda i, at: (at[n_copies] + i, 0))
        if index is shifted_part_block:
            return pl.BlockSpec(block, lambda i, at: (0, at[n_copies] + i, 0))
        return pl.BlockSpec(block, lambda i, at: index(i))

    semaphores = [pltpu.SemaphoreType.DMA((n_copies,))] if n_copies else []
    return pl.pallas_call(
        body,
        grid_spec=pltpu.PrefetchScalarGridSpec(
            num_scalar_prefetch=1,
            grid=(steps,),
            in_specs=[anywhere] * sum(n_pieces) + [spec(block, index) for _, block, index in ins],
            out_specs=[spec(block, index) for _, _, block, index in outs],
            scratch_shapes=[pltpu.VMEM(w.shape, BF) for w in weights] + semaphores + list(scratch),
        ),
        out_shape=[jax.ShapeDtypeStruct(shape, dtype) for shape, dtype, _, _ in outs],
        compiler_params=pltpu.CompilerParams(vmem_limit_bytes=VMEM_BYTES),
        name=name,
        cost_estimate=cost(flops * share),
    )(rows_at, *[a for w in weights for a in w.arrays], *[a for a, _, _ in ins])


def pick(array, index, axis):
    return lax.dynamic_index_in_dim(array, index, axis, keepdims=False)


def total(terms):
    value = terms[0].astype(F32)
    for term in terms[1:]:
        value = value + term.astype(F32)
    return value


def split_sum(terms, order, name):
    parts, size = terms[0].shape[0], terms[0].size
    rest = terms[0].shape[1:]
    columns = terms[0].shape[-1]
    rows = size // parts // columns
    tile = rows
    while tile * columns > 2**18 and tile % 32 == 0:
        tile //= 2
    flat = [t.reshape(parts, rows, columns) for t in terms]
    wanted = len(order)

    def kernel(at, *refs):
        del at
        for j in range(wanted):
            value = refs[j][0].astype(F32)
            for i in range(1, len(terms)):
                value = value + refs[i * wanted + j][0].astype(F32)
            refs[len(terms) * wanted + j][...] = value.astype(terms[0].dtype)

    outs = pl.pallas_call(
        kernel,
        grid_spec=pltpu.PrefetchScalarGridSpec(
            num_scalar_prefetch=1,
            grid=(rows // tile,),
            in_specs=[
                pl.BlockSpec((1, tile, columns), lambda i, at, j=j: (at[j], i, 0))
                for _ in terms
                for j in range(wanted)
            ],
            out_specs=[pl.BlockSpec((tile, columns), lambda i, at: (i, 0))] * wanted,
        ),
        out_shape=[jax.ShapeDtypeStruct((rows, columns), terms[0].dtype)] * wanted,
        compiler_params=pltpu.CompilerParams(vmem_limit_bytes=VMEM_BYTES),
        name=name,
        cost_estimate=cost(0, (len(terms) + 1) * size * 2 * wanted // parts),
    )(jnp.stack(order).astype(jnp.int32), *[t for t in flat for _ in range(wanted)])
    return [out.reshape(rest) for out in outs]


class Scatter:
    def __init__(self, grid, clock, kept, sent, order):
        self.grid, self.clock, self.order = grid, clock, order
        self.own, self.got = [kept], [grid.over_core(sent)]

    def step(self):
        grid, axis, self.order = self.grid, self.order[0], self.order[1:]
        terms = self.clock(*self.own, *self.got)
        if axis == "z":
            places = [(grid.z + k) % grid.nz for k in range(grid.nz)]
            own, *parts = self.clock(*split_sum(terms, places, SUM + axis))
            self.got = [grid.along_z(part, k) for k, part in enumerate(parts, 1)]
        else:
            mine, move = (grid.y, grid.over_y) if axis == "y" else (grid.x, grid.over_x)
            own, part = self.clock(*split_sum(terms, [mine, 1 - mine], SUM + axis))
            self.got = [move(part)]
        self.own = [own]

    def result(self):
        return total(self.own + self.got)


class Summed:
    def __init__(self, value):
        self.value, self.own = value, []

    def step(self):
        pass

    def result(self):
        return lax.psum_scatter(self.value, BOTH, scatter_dimension=0, tiled=True)


def to_whole(grid, part):
    group, count = grid.group, part.shape[0]
    if group == 1:
        return part
    place = lax.axis_index(SEQ)
    if group == 2 and count == 2:
        kept, got = pick(part, place, 0), grid.over_x(pick(part, 1 - place, 0))
        first = jnp.where(place == 0, kept, got)
        second = jnp.where(place == 0, got, kept)
        return jnp.concatenate([first, second])[None]
    if count % group == 0:
        return lax.all_to_all(part, SEQ, split_axis=0, concat_axis=1, tiled=True)
    every = lax.all_gather(part, SEQ, axis=1, tiled=True)
    return pick(every, place % count, 0)[None]


def from_whole(grid, whole, count):
    group = grid.group
    if group == 1:
        return whole
    place = lax.axis_index(SEQ)
    if group == 2 and count == 2:
        halves = whole.reshape(2, -1, whole.shape[-1])
        kept, got = pick(halves, place, 0), grid.over_x(pick(halves, 1 - place, 0))
        first = jnp.where(place == 0, kept, got)
        second = jnp.where(place == 0, got, kept)
        return jnp.stack([first, second])
    if count % group == 0:
        return lax.all_to_all(whole, SEQ, split_axis=1, concat_axis=0, tiled=True)
    every = lax.all_gather(whole[0], SEQ, axis=0)[:count]
    rows = whole.shape[1] // group
    return lax.dynamic_slice_in_dim(every, place * rows, rows, 1)


def attention_forward_kernel(q_ref, k_ref, v_ref, mask_ref, out_ref, total_ref, *, head, chunk):
    factor = head**-0.5 * math.log2(math.e)
    rows = q_ref.shape[1]
    for h in range(q_ref.shape[2] // head):
        lanes = slice(h * head, (h + 1) * head)
        keys, values = k_ref[0, :, lanes], v_ref[0, :, lanes]
        for start in range(0, rows, chunk):
            part = slice(start, start + chunk)
            scores = dot(keys, q_ref[0, part, lanes], NT)
            weights = jnp.exp2(scores * factor + mask_ref[0, :, part])
            total = jnp.sum(weights, axis=0, keepdims=True)
            summed = dot(values, weights.astype(BF), TN)
            total_ref[0, 0, h : h + 1, part] = total
            out_ref[0, part, lanes] = (summed / total).T.astype(BF)


def attention_backward_kernel(
    q_ref, k_ref, v_ref, mask_ref, grad_ref, ctx_ref, total_ref, out_ref, dk_sum, dv_sum, *, head, chunk
):
    scale = head**-0.5
    factor = scale * math.log2(math.e)
    rows = q_ref.shape[1]
    for h in range(q_ref.shape[2] // head):
        lanes = slice(h * head, (h + 1) * head)
        keys, values = k_ref[0, :, lanes], v_ref[0, :, lanes]
        keys_t = keys.T
        for start in range(0, rows, chunk):
            part = slice(start, start + chunk)
            queries = q_ref[0, part, lanes]
            scores = dot(keys, queries, NT)
            weights = jnp.exp2(scores * factor + mask_ref[0, :, part])
            inverse = 1.0 / total_ref[0, 0, h : h + 1, part]
            grad = grad_ref[0, part, lanes].astype(F32)
            product = (grad * ctx_ref[0, part, lanes].astype(F32)).T
            grad_total = -jnp.sum(product, axis=0, keepdims=True) * inverse
            grad_summed = (grad.T * inverse).astype(BF)
            grad_probs = dot(values, grad_summed)
            grad_scores = (weights * (grad_probs + grad_total)).astype(BF)
            dv_part = dot(weights.astype(BF), grad_summed, NT)
            dk_part = dot(grad_scores, queries)
            if start == 0:
                dv_sum[...] = dv_part
                dk_sum[...] = dk_part
            else:
                dv_sum[...] += dv_part
                dk_sum[...] += dk_part
            out_ref[0, 0, part, lanes] = (dot(keys_t, grad_scores).T * scale).astype(BF)
        out_ref[1, 0, :, lanes] = (dk_sum[...] * scale).astype(BF)
        out_ref[2, 0, :, lanes] = dv_sum[...].astype(BF)


def attention_specs(length, width, group):
    head = width // HEADS
    lanes = max(128, head)
    steps = width // lanes // GROUPS

    def columns(which):
        return pl.BlockSpec((1, length, lanes), lambda b, p: (b, 0, (which * GROUPS + group) * steps + p))

    own = pl.BlockSpec((1, length, lanes), lambda b, p: (b, 0, p))
    mask = pl.BlockSpec((1, length, length), lambda b, p: (b, 0, 0))
    totals = pl.BlockSpec((1, 1, lanes // head, length), lambda b, p: (b, p, 0, 0))
    return head, lanes, steps, columns, own, mask, totals


def attention_forward(qkv, mask, group):
    count, length, width = qkv.shape
    width = width // 3
    head, lanes, steps, columns, own, mask_spec, totals = attention_specs(length, width, group)
    return pl.pallas_call(
        partial(attention_forward_kernel, head=head, chunk=512),
        grid=(count, steps),
        in_specs=[columns(0), columns(1), columns(2), mask_spec],
        out_specs=[own, totals],
        out_shape=[
            jax.ShapeDtypeStruct((count, length, width // GROUPS), BF),
            jax.ShapeDtypeStruct((count, steps, lanes // head, length), F32),
        ],
        name="attention_forward",
        compiler_params=pltpu.CompilerParams(vmem_limit_bytes=VMEM_BYTES),
        cost_estimate=cost(12 * count * length * length * width // GROUPS),
    )(qkv, qkv, qkv, mask)


def attention_backward(qkv, mask, grad, context, totals_in, group):
    count, length, width = grad.shape
    head, lanes, steps, columns, own, mask_spec, totals = attention_specs(length, width, group)
    grads = pl.BlockSpec((3, 1, length, lanes), lambda b, p: (0, b, 0, p))
    return pl.pallas_call(
        partial(attention_backward_kernel, head=head, chunk=256),
        grid=(count, steps),
        in_specs=[columns(0), columns(1), columns(2), mask_spec, columns(0), own, totals],
        out_specs=grads,
        out_shape=jax.ShapeDtypeStruct((3, count, length, width // GROUPS), BF),
        scratch_shapes=[pltpu.VMEM((length, head), F32)] * 2,
        name="attention_backward",
        compiler_params=pltpu.CompilerParams(vmem_limit_bytes=VMEM_BYTES),
        cost_estimate=cost(26 * count * length * length * width * (LONG if group else SHORT)),
    )(qkv, qkv, qkv, mask, grad, context, totals_in)


def attention_mask(segments, globals_pair, randoms):
    count, blocks = randoms.shape[:2]
    length = segments.shape[1]
    numbers = jnp.arange(blocks, dtype=jnp.int32)
    chosen = jnp.any(globals_pair[:, :, None] == numbers, axis=1)
    nearby = jnp.abs(numbers[:, None] - numbers[None, :]) <= 1
    picked = jnp.any(randoms[:, :, :, None] == numbers, axis=2)
    seen = chosen[:, :, None] | chosen[:, None, :] | nearby[None] | picked
    seen = jnp.swapaxes(seen, 1, 2)[:, :, None, :, None]
    seen = jnp.broadcast_to(seen, (count, blocks, BLK, blocks, BLK)).reshape(count, length, length)
    same = segments[:, :, None] == segments[:, None, :]
    return jnp.where(seen & same, 0.0, MASKED).astype(F32)


def normalise(values):
    centred = values - jnp.mean(values, -1, keepdims=True)
    inverse = lax.rsqrt(jnp.mean(centred * centred, -1, keepdims=True) + EPSILON)
    return centred * inverse, inverse


def normalise_back(grad, values, gain):
    unit, inverse = normalise(values)
    inner = grad * gain
    grad_in = inverse * (
        inner - jnp.mean(inner, -1, keepdims=True) - unit * jnp.mean(inner * unit, -1, keepdims=True)
    )
    return grad_in, jnp.sum(grad * unit, 0, keepdims=True), jnp.sum(grad, 0, keepdims=True)


def accumulate(ref, rows):
    first = pl.program_id(0) == 0
    for j, row in enumerate(rows):

        @pl.when(first)
        def _():
            ref[j : j + 1] = row

        @pl.when(jnp.logical_not(first))
        def _():
            ref[j : j + 1] += row


def row_block(i):
    return (i, 0)


def shifted_row_block(i):
    raise NotImplementedError


def shifted_part_block(i):
    raise NotImplementedError


def fixed_block(i):
    return (0, 0)


def column_block(i):
    return (0, i)


def project_in(x, w_qkv, extra):
    rows, width = x.shape

    def kernel(_, ins, outs, weights, scratch):
        qkv, turned, params = outs
        w, small = weights

        @pl.when(pl.program_id(0) == 0)
        def _():
            params[...] = small[...].astype(F32).T[:16]

        unit, _ = normalise(ins[0][...].astype(F32))
        normed = (unit * params[0:1] + params[1:2]).astype(BF)
        turned[...] = normed.T
        for part, bias in enumerate((params[2:3], None, params[3:4])):
            columns = slice(part * width, (part + 1) * width)
            value = dot(normed, w[:, columns])
            qkv[:, columns] = (value if bias is None else value + bias).astype(BF)

    return run(
        kernel,
        [w_qkv, extra],
        [(x, (TILE, width), row_block)],
        [
            ((rows, 3 * width), BF, (TILE, 3 * width), row_block),
            ((width, rows), BF, (width, TILE), column_block),
            ((16, width), F32, (16, width), fixed_block),
        ],
        rows // TILE,
        6 * rows * width * width,
        name="project_in",
    )


def project_out(contexts, x, params, w_o):
    rows, width = x.shape

    def kernel(_, ins, outs, weights, scratch):
        x_ref, params = ins[:2]
        residual, normed, turned, context_turned = outs
        parts = [ref[...] for ref in ins[2:]]
        context = jnp.concatenate(parts, axis=1)
        context_turned[...] = context.T
        value = x_ref[...].astype(F32) + dot(context, weights[0][...]) + params[4:5]
        residual[...] = value
        unit, _ = normalise(value)
        low = (unit * params[5:6] + params[6:7]).astype(BF)
        normed[...] = low
        turned[...] = low.T

    return run(
        kernel,
        [w_o],
        [(x, (TILE, width), row_block), (params, (16, width), fixed_block)]
        + [(c, (TILE, c.shape[1]), row_block) for c in contexts],
        [
            ((rows, width), F32, (TILE, width), row_block),
            ((rows, width), BF, (TILE, width), row_block),
            ((width, rows), BF, (width, TILE), column_block),
            ((width, rows), BF, (width, TILE), column_block),
        ],
        rows // TILE,
        2 * rows * width * width,
        name="project_out",
    )


def feed_up(normed, w_up, bias):
    rows, width = normed.shape
    wide = w_up.shape[1]
    outer = math.sqrt(2 / math.pi)
    cubic = 0.044715

    def kernel(_, ins, outs, weights, scratch):
        value, slope = outs
        for start in range(0, wide, width):
            columns = slice(start, start + width)
            u = dot(ins[0][...], weights[0][:, columns]) + ins[1][:, columns]
            square = u * u
            half = 0.5 + 0.5 * jnp.tanh(u * (outer + outer * cubic * square))
            gelu = u * half
            value[:, columns] = gelu.astype(BF)
            rest = gelu * (1.0 - half) * (2 * outer + 6 * outer * cubic * square)
            slope[:, columns] = (half + rest).astype(BF)

    return run(
        kernel,
        [w_up],
        [(normed, (TILE, width), row_block), (bias, (1, wide), fixed_block)],
        [((rows, wide), BF, (TILE, wide), row_block)] * 2,
        rows // TILE,
        2 * rows * width * wide,
        name="feed_up",
    )


def feed_down(activated, slope, residual, upstream, params, w_down):
    rows, wide = activated.shape
    width = residual.shape[1]

    def kernel(_, ins, outs, weights, scratch):
        act, slope, residual, upstream, params = ins
        mixed, grad_hidden, sum_up, sum_down = outs
        w = weights[0]
        value = residual[...] + dot(act[...], w[...]) + params[7:8]
        mixed[...] = value.astype(BF)
        dy = upstream[...]
        sums = []
        for start in range(0, wide, width):
            columns = slice(start, start + width)
            grad = dot(dy, w[columns, :], NT).astype(BF).astype(F32)
            low = (grad * slope[:, columns].astype(F32)).astype(BF)
            grad_hidden[:, columns] = low
            sums.append(jnp.sum(low.astype(F32), 0, keepdims=True))
        accumulate(sum_up, [jnp.concatenate(sums, axis=1)])
        accumulate(sum_down, [jnp.sum(dy.astype(F32), 0, keepdims=True)])

    return run(
        kernel,
        [w_down],
        [
            (activated, (TILE, wide), row_block),
            (slope, (TILE, wide), row_block),
            (residual, (TILE, width), row_block),
            (upstream, (TILE, width), row_block),
            (params, (16, width), fixed_block),
        ],
        [
            ((rows, width), BF, (TILE, width), row_block),
            ((rows, wide), BF, (TILE, wide), row_block),
            ((8, wide), F32, (8, wide), fixed_block),
            ((8, width), F32, (8, width), fixed_block),
        ],
        rows // TILE,
        4 * rows * width * wide,
        name="feed_down",
        share=LONG,
    )


def feed_back(grad_hidden, residual, upstream, params, w_up, w_o):
    rows, width = residual.shape
    wide = grad_hidden.shape[1]

    def kernel(_, ins, outs, weights, scratch):
        du, residual, upstream, params = ins
        grad_residual, grad_att, grad_context, sums = outs
        grad = dot(du[...], weights[0][...], NT)
        part, gain, shift = normalise_back(grad, residual[...], params[5:6])
        total = upstream[...].astype(F32) + part
        grad_residual[...] = total
        low = total.astype(BF)
        grad_att[...] = low
        grad_context[...] = dot(low, weights[1][...], NT).astype(BF)
        accumulate(sums, [jnp.sum(low.astype(F32), 0, keepdims=True), gain, shift])

    return run(
        kernel,
        [w_up, w_o],
        [
            (grad_hidden, (TILE, wide), row_block),
            (residual, (TILE, width), row_block),
            (upstream, (TILE, width), row_block),
            (params, (16, width), fixed_block),
        ],
        [
            ((rows, width), F32, (TILE, width), row_block),
            ((rows, width), BF, (TILE, width), row_block),
            ((rows, width), BF, (TILE, width), row_block),
            ((8, width), F32, (8, width), fixed_block),
        ],
        rows // TILE,
        2 * rows * width * (wide + width),
        name="feed_back",
        share=LONG,
    )


def project_back(grads, grad_residual, x, params, w_qkv, first, count):
    width = x.shape[1]
    each = width // GROUPS

    def kernel(_, ins, outs, weights, scratch):
        grad_residual, x_ref, params = ins[:3]
        grad_in, sums = outs
        w = weights[0]
        grad = None
        biases = []
        for part in range(3):
            cut = [ref[part] for ref in ins[3:]]
            low = jnp.concatenate(cut, axis=1)
            if part != 1:
                biases.append(jnp.sum(low.astype(F32), 0, keepdims=True))
            value = dot(low, w[:, part * width : (part + 1) * width], NT)
            grad = value if grad is None else grad + value
        part, gain, shift = normalise_back(grad, x_ref[...].astype(F32), params[0:1])
        grad_in[...] = (grad_residual[...] + part).astype(BF)
        accumulate(sums, [gain, shift] + biases)

    return run(
        kernel,
        [w_qkv],
        [
            (grad_residual, (TILE, width), shifted_row_block),
            (x, (TILE, width), shifted_row_block),
            (params, (16, width), fixed_block),
        ]
        + [(g, (3, TILE, each), shifted_part_block) for g in grads],
        [
            ((count * TILE, width), BF, (TILE, width), row_block),
            ((8, width), F32, (8, width), fixed_block),
        ],
        count,
        6 * count * TILE * width * width,
        scalars=[first],
        name="project_back",
    )


def weight_grad(grid, clock, pairs, order):
    if not grid.cube:
        return Summed(jnp.concatenate([dot(turned, part) for turned, right in pairs for part in right], axis=1))
    features, rows = pairs[0][0].shape
    tile = min(512, *(right.shape[2] for _, right in pairs))
    counts = [right.shape[0] * right.shape[2] // tile for _, right in pairs]
    columns = sum(counts) * tile
    shard = features // grid.nz // 8
    places, shape = leading(grid, order)

    def kernel(scalars, ins, outs, weights, scratch):
        first = scalars[0] == 0
        step = pl.program_id(0)

        def work(turned, right, low, high):
            value = dot(turned[...], right[0]).astype(BF)
            for (z, y, x), at in places:
                start = ((z * 2 + y) * 4 + x) * shard
                low[at * shard : (at + 1) * shard] = value[start : start + shard]
                start += 2 * shard
                high[at * shard : (at + 1) * shard] = value[start : start + shard]

        done = 0
        for j, count in enumerate(counts):
            here = (step >= done) & (step < done + count)
            done += count

            @pl.when(here & first)
            def _():
                work(ins[2 * j], ins[2 * j + 1], *outs)

            @pl.when(here & jnp.logical_not(first))
            def _():
                work(ins[2 * j], ins[2 * j + 1], outs[1], outs[0])

    ins, done = [], 0
    for (turned, right), count in zip(pairs, counts):
        per = right.shape[2] // tile

        def block(i, done=done, count=count, per=per):
            j = jnp.clip(i - done, 0, count - 1)
            return (j // per, 0, j % per)

        turned, right = clock(turned, right)
        ins += [(turned, (features, rows), fixed_block), (right, (1, rows, tile), block)]
        done += count
    kept, sent = run(
        kernel,
        [],
        ins,
        [((features // 2, columns), BF, (features // 2, tile), column_block)] * 2,
        sum(counts),
        2 * rows * features * columns,
        scalars=[grid.core],
        name=WG + str(columns),
    )
    shape += (shard, columns)
    kept, sent = clock(kept, sent)
    return Scatter(grid, clock, kept.reshape(shape), sent.reshape(shape), order)


def weight_grad_turned(grid, clock, turned, right, order):
    features, rows = turned.shape
    each = right.shape[1] // (grid.nz * 8)
    places, shape = leading(grid, order)

    def kernel(scalars, ins, outs, weights, scratch):
        first = scalars[0] == 0
        value = dot(ins[0][...], ins[1][...]).astype(BF)

        def store(low, high):
            for (z, y, x), at in places:
                start = ((z * 2 + y) * 4 + x) * each
                low[at] = value[:, start : start + each]
                start += 2 * each
                high[at] = value[:, start : start + each]

        @pl.when(first)
        def _():
            store(*outs)

        @pl.when(jnp.logical_not(first))
        def _():
            store(outs[1], outs[0])

    tile = min(256, features)
    shape += (features, each)
    turned, right = clock(turned, right)
    kept, sent = run(
        kernel,
        [],
        [(turned, (tile, rows), row_block), (right, right.shape, fixed_block)],
        [((grid.nz * 4, features, each), BF, (grid.nz * 4, tile, each), lambda i: (0, i, 0))] * 2,
        features // tile,
        2 * rows * features * right.shape[1],
        scalars=[grid.core],
        name=WG + "turned",
    )
    kept, sent = clock(kept, sent)
    return Scatter(grid, clock, kept.reshape(shape), sent.reshape(shape), order)


def leading(grid, order):
    counts = {"z": grid.nz, "y": 2, "x": 2}
    places = []
    for z in range(grid.nz):
        for y in range(2):
            for x in range(2):
                here = {"z": z, "y": y, "x": x}
                at = 0
                for axis in order:
                    at = at * counts[axis] + here[axis]
                places.append(((z, y, x), at))
    return places, tuple(counts[axis] for axis in order)


def shards(tokens, cotangent, segments, global_blocks, random_blocks, *params):
    grid = Grid()
    gain1, shift1, w_q, b_q, w_k, w_v, b_v, w_o, b_o, gain2, shift2, w_up, b_up, w_down, b_down = params
    count = tokens.shape[0]
    width = tokens.shape[-1]
    wide = w_up.shape[1]
    each = w_v.shape[0]
    devices = grid.dp * grid.group
    replicas = max(1, grid.group // count)

    inputs = to_whole(grid, tokens)
    n, length = inputs.shape[:2]
    rows = n * length
    inputs = inputs.reshape(rows, width)
    vectors = [gain1, shift1, b_q, b_v, b_o, gain2, shift2, b_down]
    extra = jnp.concatenate([*vectors, b_up]).reshape(-1, each).T
    extra = jnp.pad(extra, ((0, 0), (0, 128 - extra.shape[1])))

    clock = Clock()
    first = gather(jnp.concatenate([w_q, w_k], axis=1))
    second = Gather(grid, jnp.concatenate([w_v, w_o, extra], axis=1))
    inputs = second.near(clock, inputs)
    third = Gather(grid, w_up)
    fourth = gather(w_down)
    if grid.group > 1:
        place = lax.axis_index(SEQ)
        start = place * n if count % grid.group == 0 else place % count
        segments, global_blocks, random_blocks = (
            lax.dynamic_slice_in_dim(a, start, n, 0) for a in (segments, global_blocks, random_blocks)
        )
    mask = attention_mask(segments, global_blocks, random_blocks)

    second = second.pieces(clock)
    inputs = third.near(clock, inputs)
    w_qkv = columns_of((first, 0, 2 * width), (second, 0, width))
    w_o, extra = columns_of((second, width, width)), columns_of((second, 2 * width, 128))
    inputs = clock(inputs)
    qkv, normed1_turned, params = clock(*project_in(inputs, w_qkv, extra))
    qkv = qkv.reshape(n, length, 3 * width)
    upstream = to_whole(grid, clock(cotangent)).reshape(rows, width)
    attended = []
    for g in range(GROUPS):
        qkv, mask = clock(qkv, mask)
        attended.append(clock(*attention_forward(qkv, mask, g)))
    contexts = [a[0].reshape(rows, -1) for a in attended]
    w_up, w_down = columns_of((third.pieces(clock), 0, wide)), columns_of((fourth, 0, width))
    contexts[0] = clock(contexts[0])
    residual, normed2, normed2_turned, context_turned = clock(*project_out(contexts, inputs, params, w_o))
    bias_up = params[8 : 8 + wide // width].reshape(-1, devices, each).transpose(1, 0, 2).reshape(1, -1)
    activated, slope = clock(*feed_up(normed2, w_up, bias_up))

    upstream_turned = upstream.T
    if grid.cube:
        sum_w_down = weight_grad_turned(grid, clock, upstream_turned, activated, "yzx")
    else:
        sum_w_down = Summed(dot(activated, upstream, TN))
    activated = clock(activated)
    mixed, grad_hidden, sum_up, sum_down = clock(
        *feed_down(activated, slope, residual, upstream, params, w_down)
    )
    mixed = from_whole(grid, mixed.reshape(n, length, width), count)
    sum_w_down.step()
    sum_w_up = weight_grad(grid, clock, [(normed2_turned, grad_hidden[None])], "xyz")
    grad_hidden = clock(grad_hidden)
    grad_residual, grad_att, grad_context, sums2 = clock(
        *feed_back(grad_hidden, residual, upstream, params, w_up, w_o)
    )
    sum_w_down.step()
    sum_w_up.step()
    grad_context = grad_context.reshape(n, length, width)
    grads, sums_qkv = [], []
    for g in range(GROUPS):
        grad_context = clock(grad_context)
        grad = clock(attention_backward(qkv, mask, grad_context, *attended[g], g)).reshape(3, rows, -1)
        grads.append(grad)
        if g > 0:
            sum_w_up.step()
            sums_qkv[0].step()
        pairs = [(normed1_turned, grad)] + [(context_turned, grad_att[None])] * (g == 0)
        sums_qkv.append(weight_grad(grid, clock, pairs, "yxz" if g == 0 else "xyz"))
        if g == 0:
            sum_w_down.step()
            sum_w_up.step()
    steps = rows // TILE
    swap = grid.group == 2 and count == 2
    half = steps // 2 if swap else steps
    place = lax.axis_index(SEQ)
    grads[-1] = clock(grads[-1])
    grad_inputs, sums1 = clock(
        *project_back(grads, grad_residual, inputs, params, w_qkv, (1 - place) * half if swap else 0, half)
    )
    sums_qkv[0].step()
    sums_qkv[1].step()
    if swap:
        got = grid.over_x(grad_inputs)
        grads[-1] = clock(grads[-1])
        own, more = clock(*project_back(grads, grad_residual, inputs, params, w_qkv, place * half, half))
        sums1 = sums1 + more
        grad_inputs = jnp.stack([jnp.where(place == 0, own, got), jnp.where(place == 0, got, own)])
    else:
        grad_inputs = from_whole(grid, grad_inputs.reshape(n, length, width), count)
    sums_qkv[0].step()
    sums_qkv[1].step()
    sums1, sums2, sum_up, sum_down = clock(sums1, sums2, sum_up, sum_down)
    vectors = jnp.concatenate([sums1[:4], sums2[:3], sum_down[:1]])
    vectors = vectors.reshape(8, devices, each).transpose(1, 0, 2).reshape(devices, -1)
    vectors = jnp.concatenate([vectors, sum_up[:1].reshape(devices, -1)], axis=1)
    if grid.cube:
        vectors = vectors.reshape(grid.nz, 2, 2, 2, -1, 128)
        vectors = halve(vectors, grid.core, 2, grid.over_core)
        vectors = halve(vectors, grid.y, 1, grid.over_y)
        sums_qkv[1].step()
        vectors = halve(clock(vectors), grid.x, 1, grid.over_x)
        parts = [pick(vectors, (grid.z + k) % grid.nz, 0) for k in range(grid.nz)]
        vectors = total(parts[:1] + [grid.along_z(part, k) for k, part in enumerate(parts) if k])
    else:
        vectors = lax.psum_scatter(vectors, BOTH, scatter_dimension=0, tiled=True)
    vectors = vectors + clock.token[0, 0]

    share = 1.0 / replicas
    grad_w_down = sum_w_down.result() * share
    if grid.cube:
        grad_w_down = grad_w_down.T
    grad_w_up = sum_w_up.result() * share
    ended = [moving.result() * share for moving in sums_qkv]
    cut = width // GROUPS
    grad_w_o = ended[0][:, 3 * cut :]
    grad_w_q, grad_w_k, grad_w_v = (
        jnp.concatenate([e[:, j * cut : (j + 1) * cut] for e in ended], axis=1) for j in range(3)
    )
    vectors = (vectors * share).reshape(-1)
    grad_b_up = vectors[8 * each :]
    grad_gain1, grad_shift1, grad_b_q, grad_b_v, grad_b_o, grad_gain2, grad_shift2, grad_b_down = (
        vectors[j * each : (j + 1) * each] for j in range(8)
    )
    return (
        mixed, grad_inputs, grad_gain1, grad_shift1, grad_w_q, grad_b_q, grad_w_k, grad_w_v, grad_b_v,
        grad_w_o, grad_b_o, grad_gain2, grad_shift2, grad_w_up, grad_b_up, grad_w_down, grad_b_down,
    )


def halve(value, mine, dim, move):
    return pick(value, mine, dim) + move(pick(value, 1 - mine, dim))


def solution(mesh):
    rows = P(DP, SEQ, None)
    vector, matrix = P(BOTH), P(BOTH, None)
    params = (
        vector, vector, matrix, vector, matrix, matrix, vector, matrix, vector, vector, vector, matrix,
        vector, matrix, vector,
    )
    in_specs = (rows, rows, P(DP, None), P(DP, None), P(DP, None, None)) + params
    out_specs = (rows, rows) + params
    return jax.shard_map(shards, mesh=mesh, in_specs=in_specs, out_specs=out_specs, check_vma=False)
```

```python
from functools import partial
import math

import jax
import jax.numpy as jnp
from jax import lax
from jax.experimental import pallas as pl
from jax.experimental.pallas import tpu as pltpu
from jax.sharding import PartitionSpec as P

HEADS = 16
BLK = 64
EPSILON = 1e-06
MASKED = -1e30
DP, SEQ = "dp", "seq"
BOTH = (DP, SEQ)
BF, F32 = jnp.bfloat16, jnp.float32
NT = (((1,), (1,)), ((), ()))
NN = (((1,), (0,)), ((), ()))
TN = (((0,), (0,)), ((), ()))
VMEM_BYTES = 60 * 2**20
TILE = 256
GROUPS = 2
LONG, SHORT = 5.0, 0.05
WG, SUM = "weight_grad_", "sum_"


def cost(flops):
    return pl.CostEstimate(flops=int(flops), bytes_accessed=0, transcendentals=0)


def dot(left, right, dims=NN):
    return lax.dot_general(left, right, dims, preferred_element_type=F32)


class Grid:
    def __init__(self):
        self.dp = lax.axis_size(DP)
        self.group = lax.axis_size(SEQ)
        self.cube = self.group == 2 and self.dp % 4 == 0
        if self.cube:
            self.nz = self.dp // 4
            place = lax.axis_index(DP)
            self.x = lax.axis_index(SEQ)
            self.z, self.y, self.core = place // 4, place // 2 % 2, place % 2

    def over_x(self, v):
        return lax.ppermute(v, SEQ, [(0, 1), (1, 0)])

    def over_y(self, v):
        return lax.ppermute(v, DP, [(i, i ^ 2) for i in range(self.dp)])

    def over_xy(self, v):
        pairs = [(2 * i + x, 2 * (i ^ 2) + 1 - x) for i in range(self.dp) for x in range(2)]
        return lax.ppermute(v, BOTH, pairs)

    def over_core(self, v):
        return lax.ppermute(v, DP, [(i, i ^ 1) for i in range(self.dp)])

    def along_z(self, v, k):
        return lax.ppermute(v, DP, [(i, (i + 4 * k) % self.dp) for i in range(self.dp)])

    def device(self, c, y, x, k):
        z = (self.z - k) % self.nz
        return ((z * 2 + (self.y ^ y)) * 2 + (self.core ^ c)) * 2 + (self.x ^ x)


class Weight:
    def __init__(self, shape):
        self.shape, self.arrays, self.copies, self.rows_at = shape, [], [], []

    def add(self, array, index, rows, row, source=0, width=None, target=0):
        for i, known in enumerate(self.arrays):
            if known is array:
                break
        else:
            i = len(self.arrays)
            self.arrays.append(array)
        self.copies.append((i, index, rows, source, width or array.shape[-1], target))
        self.rows_at.append(row)


def whole_weight(array):
    weight = Weight(array.shape)
    weight.add(array, None, array.shape[0], 0)
    return weight


def columns_of(*parts):
    pieces = parts[0][0]
    weight = Weight((len(pieces) * pieces[0][0].shape[1], sum(width for _, _, width in parts)))
    target = 0
    for pieces, start, width in parts:
        for array, index, device in pieces:
            rows = array.shape[1]
            weight.add(array, index, rows, device * rows, start, width, target)
        target += width
    return weight


def gather(shard):
    every = lax.all_gather(shard, BOTH, axis=0)
    return [(every, i, i) for i in range(every.shape[0])]


class Gather:
    def __init__(self, grid, shard):
        self.grid = grid
        if not grid.cube:
            self.all = gather(shard)
            return
        shard = shard[None]
        self.got = [shard] + [grid.along_z(shard, k) for k in range(1, grid.nz)]

    def near(self, clock, wait):
        if not self.grid.cube:
            return wait
        own = jnp.concatenate(self.got)
        own, wait = clock(own, wait)
        self.got = [own, self.grid.over_xy(own), self.grid.over_x(own), self.grid.over_y(own)]
        return wait

    def pieces(self, clock):
        grid = self.grid
        if not grid.cube:
            return self.all
        self.got = clock(*self.got)
        pieces = []
        for (y, x), piece in zip(((0, 0), (1, 1), (0, 1), (1, 0)), self.got):
            for c, array in enumerate((piece, grid.over_core(piece))):
                pieces += [(array, k, grid.device(c, y, x, k)) for k in range(grid.nz)]
        return pieces


class Clock:
    def __init__(self):
        self.token = None

    def __call__(self, *values):
        if self.token is None:
            self.token = jnp.zeros((8, 128), F32)
        *values, self.token = lax.optimization_barrier((*values, self.token))
        return values[0] if len(values) == 1 else values


def run(kernel, weights, ins, outs, steps, flops, scratch=(), scalars=(), name=None, share=SHORT, stages=1):
    rows_at = [row for w in weights for row in w.rows_at] + list(scalars)
    rows_at = jnp.stack([jnp.asarray(row, jnp.int32) for row in rows_at] or [jnp.int32(0)])
    moves = []
    for which, w in enumerate(weights):
        cut = w.shape[1] // stages
        for n, (i, index, rows, source, width, target) in enumerate(w.copies):
            at = target
            while at < target + width:
                size = min(cut - at % cut, target + width - at)
                moves.append((at // cut, which, n, (i, index, rows, source + at - target, size, at)))
                at += size
    moves.sort(key=lambda move: move[0])
    bases = [sum(len(w.copies) for w in weights[:j]) for j in range(len(weights))]
    n_copies = sum(len(w.copies) for w in weights)
    n_pieces = [len(w.arrays) for w in weights]

    def body(at, *refs):
        refs = list(refs)

        def take(count):
            taken, refs[:count] = refs[:count], []
            return taken

        piece_refs = [take(count) for count in n_pieces]
        in_refs, out_refs = take(len(ins)), take(len(outs))
        held = take(len(weights))
        sems = take(1)[0] if moves else None

        def copies(stage=None):
            for n, (due, which, row, (i, index, rows, source, width, target)) in enumerate(moves):
                if stage is None or due == stage:
                    ref = piece_refs[which][i] if index is None else piece_refs[which][i].at[index]
                    yield pltpu.make_async_copy(
                        ref.at[:, pl.ds(source, width)],
                        held[which].at[pl.ds(pl.multiple_of(at[bases[which] + row], rows), rows), pl.ds(target, width)],
                        sems.at[n],
                    )

        step = pl.program_id(0)
        if moves:

            @pl.when(step == 0)
            def _():
                for copy in copies():
                    copy.start()

            for stage in range(stages):

                @pl.when(step == stage * (steps // stages))
                def _():
                    for copy in copies(stage):
                        copy.wait()

        values = [at[n_copies + i] for i in range(len(scalars))]
        kernel(values, in_refs, out_refs, held, refs)

    anywhere = pl.BlockSpec(memory_space=pl.ANY)

    def spec(block, index):
        if index is shifted_row_block:
            return pl.BlockSpec(block, lambda i, at: (at[n_copies] + i, 0))
        if index is shifted_part_block:
            return pl.BlockSpec(block, lambda i, at: (0, at[n_copies] + i, 0))
        return pl.BlockSpec(block, lambda i, at: index(i))

    semaphores = [pltpu.SemaphoreType.DMA((len(moves),))] if moves else []
    return pl.pallas_call(
        body,
        grid_spec=pltpu.PrefetchScalarGridSpec(
            num_scalar_prefetch=1,
            grid=(steps,),
            in_specs=[anywhere] * sum(n_pieces) + [spec(block, index) for _, block, index in ins],
            out_specs=[spec(block, index) for _, _, block, index in outs],
            scratch_shapes=[pltpu.VMEM(w.shape, BF) for w in weights] + semaphores + list(scratch),
        ),
        out_shape=[jax.ShapeDtypeStruct(shape, dtype) for shape, dtype, _, _ in outs],
        compiler_params=pltpu.CompilerParams(vmem_limit_bytes=VMEM_BYTES),
        name=name,
        cost_estimate=cost(flops * share),
    )(rows_at, *[a for w in weights for a in w.arrays], *[a for a, _, _ in ins])


def pick(array, index, axis):
    return lax.dynamic_index_in_dim(array, index, axis, keepdims=False)


def total(terms):
    value = terms[0].astype(F32)
    for term in terms[1:]:
        value = value + term.astype(F32)
    return value


def split_sum(terms, order, name, share):
    parts, size = terms[0].shape[0], terms[0].size
    rest = terms[0].shape[1:]
    columns = terms[0].shape[-1]
    rows = size // parts // columns
    tile = rows
    while tile * columns > 2**18 and tile % 32 == 0:
        tile //= 2
    flat = [t.reshape(parts, rows, columns) for t in terms]
    wanted = len(order)

    def kernel(at, *refs):
        del at
        for j in range(wanted):
            value = refs[j][0].astype(F32)
            for i in range(1, len(terms)):
                value = value + refs[i * wanted + j][0].astype(F32)
            refs[len(terms) * wanted + j][...] = value.astype(terms[0].dtype)

    outs = pl.pallas_call(
        kernel,
        grid_spec=pltpu.PrefetchScalarGridSpec(
            num_scalar_prefetch=1,
            grid=(rows // tile,),
            in_specs=[
                pl.BlockSpec((1, tile, columns), lambda i, at, j=j: (at[j], i, 0))
                for _ in terms
                for j in range(wanted)
            ],
            out_specs=[pl.BlockSpec((tile, columns), lambda i, at: (i, 0))] * wanted,
        ),
        out_shape=[jax.ShapeDtypeStruct((rows, columns), terms[0].dtype)] * wanted,
        compiler_params=pltpu.CompilerParams(vmem_limit_bytes=VMEM_BYTES),
        name=name,
        cost_estimate=cost(2e10 * share),
    )(jnp.stack(order).astype(jnp.int32), *[t for t in flat for _ in range(wanted)])
    return [out.reshape(rest) for out in outs]


class Scatter:
    def __init__(self, grid, clock, kept, sent, order):
        self.grid, self.clock, self.order = grid, clock, order
        self.own, self.got = [kept], [grid.over_core(sent)]

    def step(self, share=SHORT):
        grid, axis, self.order = self.grid, self.order[0], self.order[1:]
        terms = self.clock(*self.own, *self.got)
        if axis == "z":
            places = [(grid.z + k) % grid.nz for k in range(grid.nz)]
            own, *parts = self.clock(*split_sum(terms, places, SUM + axis, share))
            self.got = [grid.along_z(part, k) for k, part in enumerate(parts, 1)]
        else:
            mine, move = (grid.y, grid.over_y) if axis == "y" else (grid.x, grid.over_x)
            own, part = self.clock(*split_sum(terms, [mine, 1 - mine], SUM + axis, share))
            self.got = [move(part)]
        self.own = [own]

    def wait(self, clock):
        if self.got:
            self.got = list(clock(*self.got))

    def result(self):
        return total(self.own + self.got)


class Summed:
    def __init__(self, value):
        self.value, self.own = value, []

    def step(self, share=SHORT):
        pass

    def wait(self, clock):
        pass

    def result(self):
        return lax.psum_scatter(self.value, BOTH, scatter_dimension=0, tiled=True)


def to_whole(grid, part):
    group, count = grid.group, part.shape[0]
    if group == 1:
        return part
    place = lax.axis_index(SEQ)
    if group == 2 and count == 2:
        kept, got = pick(part, place, 0), grid.over_x(pick(part, 1 - place, 0))
        first = jnp.where(place == 0, kept, got)
        second = jnp.where(place == 0, got, kept)
        return jnp.concatenate([first, second])[None]
    if count % group == 0:
        return lax.all_to_all(part, SEQ, split_axis=0, concat_axis=1, tiled=True)
    every = lax.all_gather(part, SEQ, axis=1, tiled=True)
    return pick(every, place % count, 0)[None]


class FromWhole:
    def __init__(self, grid, clock, whole, count):
        self.grid, self.clock, self.whole, self.count = grid, clock, whole, count
        self.swap = grid.group == 2 and count == 2
        if self.swap:
            place = lax.axis_index(SEQ)
            halves = whole.reshape(2, -1, whole.shape[-1])
            self.kept, self.got = pick(halves, place, 0), grid.over_x(pick(halves, 1 - place, 0))

    def result(self):
        group, whole, count = self.grid.group, self.whole, self.count
        place = lax.axis_index(SEQ)
        if self.swap:
            got = self.clock(self.got)
            return jnp.stack([jnp.where(place == 0, self.kept, got), jnp.where(place == 0, got, self.kept)])
        if group == 1:
            return whole
        if count % group == 0:
            return lax.all_to_all(whole, SEQ, split_axis=1, concat_axis=0, tiled=True)
        every = lax.all_gather(whole[0], SEQ, axis=0)[:count]
        rows = whole.shape[1] // group
        return lax.dynamic_slice_in_dim(every, place * rows, rows, 1)


def attention_forward_kernel(
    q_ref, k_ref, v_ref, mask_ref, out_ref, total_ref, weight_ref, *, head, chunk
):
    factor = head**-0.5 * math.log2(math.e)
    rows = q_ref.shape[1]
    for h in range(q_ref.shape[2] // head):
        lanes = slice(h * head, (h + 1) * head)
        keys, values = k_ref[0, :, lanes], v_ref[0, :, lanes]
        for start in range(0, rows, chunk):
            part = slice(start, start + chunk)
            scores = dot(keys, q_ref[0, part, lanes], NT)
            weights = jnp.exp2(scores * factor + mask_ref[0, :, part])
            total = jnp.sum(weights, axis=0, keepdims=True)
            low = weights.astype(BF)
            weight_ref[0, 0, h, :, part] = low
            summed = dot(values, low, TN)
            total_ref[0, 0, h : h + 1, part] = total
            out_ref[0, part, lanes] = (summed / total).T.astype(BF)


def attention_backward_kernel(
    q_ref, k_ref, v_ref, weight_ref, grad_ref, ctx_ref, total_ref, out_ref, dk_sum, dv_sum, *, head, chunk
):
    scale = head**-0.5
    rows = q_ref.shape[1]
    for h in range(q_ref.shape[2] // head):
        lanes = slice(h * head, (h + 1) * head)
        keys, values = k_ref[0, :, lanes], v_ref[0, :, lanes]
        keys_t = keys.T
        for start in range(0, rows, chunk):
            part = slice(start, start + chunk)
            queries = q_ref[0, part, lanes]
            low = weight_ref[0, 0, h, :, part]
            inverse = 1.0 / total_ref[0, 0, h : h + 1, part]
            grad = grad_ref[0, part, lanes].astype(F32)
            product = (grad * ctx_ref[0, part, lanes].astype(F32)).T
            grad_total = -jnp.sum(product, axis=0, keepdims=True) * inverse
            grad_summed = (grad.T * inverse).astype(BF)
            grad_probs = dot(values, grad_summed)
            grad_scores = (low.astype(F32) * (grad_probs + grad_total)).astype(BF)
            dv_part = dot(low, grad_summed, NT)
            dk_part = dot(grad_scores, queries)
            if start == 0:
                dv_sum[...] = dv_part
                dk_sum[...] = dk_part
            else:
                dv_sum[...] += dv_part
                dk_sum[...] += dk_part
            out_ref[0, 0, part, lanes] = (dot(keys_t, grad_scores).T * scale).astype(BF)
        out_ref[1, 0, :, lanes] = (dk_sum[...] * scale).astype(BF)
        out_ref[2, 0, :, lanes] = dv_sum[...].astype(BF)


def attention_specs(length, width, group):
    head = width // HEADS
    lanes = max(128, head)
    steps = width // lanes // GROUPS

    def columns(which):
        return pl.BlockSpec((1, length, lanes), lambda b, p: (b, 0, (which * GROUPS + group) * steps + p))

    own = pl.BlockSpec((1, length, lanes), lambda b, p: (b, 0, p))
    mask = pl.BlockSpec((1, length, length), lambda b, p: (b, 0, 0))
    totals = pl.BlockSpec((1, 1, lanes // head, length), lambda b, p: (b, p, 0, 0))
    weights = pl.BlockSpec((1, 1, lanes // head, length, length), lambda b, p: (b, p, 0, 0, 0))
    return head, lanes, steps, columns, own, mask, totals, weights


def attention_forward(qkv, mask, group):
    count, length, width = qkv.shape
    width = width // 3
    head, lanes, steps, columns, own, mask_spec, totals, weights = attention_specs(length, width, group)
    return pl.pallas_call(
        partial(attention_forward_kernel, head=head, chunk=512),
        grid=(count, steps),
        in_specs=[columns(0), columns(1), columns(2), mask_spec],
        out_specs=[own, totals, weights],
        out_shape=[
            jax.ShapeDtypeStruct((count, length, width // GROUPS), BF),
            jax.ShapeDtypeStruct((count, steps, lanes // head, length), F32),
            jax.ShapeDtypeStruct((count, steps, lanes // head, length, length), BF),
        ],
        name="attention_forward",
        compiler_params=pltpu.CompilerParams(vmem_limit_bytes=VMEM_BYTES),
        cost_estimate=cost(12 * count * length * length * width // GROUPS),
    )(qkv, qkv, qkv, mask)


def attention_backward(qkv, grad, context, totals_in, weights_in, group):
    count, length, width = grad.shape
    head, lanes, steps, columns, own, mask_spec, totals, weights = attention_specs(length, width, group)
    grads = pl.BlockSpec((3, 1, length, lanes), lambda b, p: (0, b, 0, p))
    return pl.pallas_call(
        partial(attention_backward_kernel, head=head, chunk=256),
        grid=(count, steps),
        in_specs=[columns(0), columns(1), columns(2), weights, columns(0), own, totals],
        out_specs=grads,
        out_shape=jax.ShapeDtypeStruct((3, count, length, width // GROUPS), BF),
        scratch_shapes=[pltpu.VMEM((length, head), F32)] * 2,
        name="attention_backward",
        compiler_params=pltpu.CompilerParams(vmem_limit_bytes=VMEM_BYTES),
        cost_estimate=cost(26 * count * length * length * width * (LONG if group else SHORT)),
    )(qkv, qkv, qkv, weights_in, grad, context, totals_in)


def attention_mask(segments, globals_pair, randoms):
    count, blocks = randoms.shape[:2]
    length = segments.shape[1]
    numbers = jnp.arange(blocks, dtype=jnp.int32)
    chosen = jnp.any(globals_pair[:, :, None] == numbers, axis=1)
    nearby = jnp.abs(numbers[:, None] - numbers[None, :]) <= 1
    picked = jnp.any(randoms[:, :, :, None] == numbers, axis=2)
    seen = chosen[:, :, None] | chosen[:, None, :] | nearby[None] | picked
    seen = jnp.swapaxes(seen, 1, 2)[:, :, None, :, None]
    seen = jnp.broadcast_to(seen, (count, blocks, BLK, blocks, BLK)).reshape(count, length, length)
    same = segments[:, :, None] == segments[:, None, :]
    return jnp.where(seen & same, 0.0, MASKED).astype(F32)


def normalise(values):
    centred = values - jnp.mean(values, -1, keepdims=True)
    inverse = lax.rsqrt(jnp.mean(centred * centred, -1, keepdims=True) + EPSILON)
    return centred * inverse, inverse


def normalise_back(grad, values, gain):
    unit, inverse = normalise(values)
    inner = grad * gain
    grad_in = inverse * (
        inner - jnp.mean(inner, -1, keepdims=True) - unit * jnp.mean(inner * unit, -1, keepdims=True)
    )
    return grad_in, jnp.sum(grad * unit, 0, keepdims=True), jnp.sum(grad, 0, keepdims=True)


def accumulate(ref, rows):
    first = pl.program_id(0) == 0
    for j, row in enumerate(rows):

        @pl.when(first)
        def _():
            ref[j : j + 1] = row

        @pl.when(jnp.logical_not(first))
        def _():
            ref[j : j + 1] += row


def row_block(i):
    return (i, 0)


def shifted_row_block(i):
    raise NotImplementedError


def shifted_part_block(i):
    raise NotImplementedError


def fixed_block(i):
    return (0, 0)


def column_block(i):
    return (0, i)


def project_in(x, w_qkv, extra):
    rows, width = x.shape

    def kernel(_, ins, outs, weights, scratch):
        qkv, turned, params = outs
        w, small = weights

        @pl.when(pl.program_id(0) == 0)
        def _():
            params[...] = small[...].astype(F32).T[:16]

        unit, _ = normalise(ins[0][...].astype(F32))
        normed = (unit * params[0:1] + params[1:2]).astype(BF)
        turned[...] = normed.T
        for part, bias in enumerate((params[2:3], None, params[3:4])):
            columns = slice(part * width, (part + 1) * width)
            value = dot(normed, w[:, columns])
            qkv[:, columns] = (value if bias is None else value + bias).astype(BF)

    return run(
        kernel,
        [w_qkv, extra],
        [(x, (TILE, width), row_block)],
        [
            ((rows, 3 * width), BF, (TILE, 3 * width), row_block),
            ((width, rows), BF, (width, TILE), column_block),
            ((16, width), F32, (16, width), fixed_block),
        ],
        rows // TILE,
        6 * rows * width * width,
        name="project_in",
    )


def project_out(contexts, x, params, w_o):
    rows, width = x.shape

    def kernel(_, ins, outs, weights, scratch):
        x_ref, params = ins[:2]
        residual, normed, turned, context_turned = outs
        parts = [ref[...] for ref in ins[2:]]
        context = jnp.concatenate(parts, axis=1)
        context_turned[...] = context.T
        value = x_ref[...].astype(F32) + dot(context, weights[0][...]) + params[4:5]
        residual[...] = value
        unit, _ = normalise(value)
        low = (unit * params[5:6] + params[6:7]).astype(BF)
        normed[...] = low
        turned[...] = low.T

    return run(
        kernel,
        [w_o],
        [(x, (TILE, width), row_block), (params, (16, width), fixed_block)]
        + [(c, (TILE, c.shape[1]), row_block) for c in contexts],
        [
            ((rows, width), F32, (TILE, width), row_block),
            ((rows, width), BF, (TILE, width), row_block),
            ((width, rows), BF, (width, TILE), column_block),
            ((width, rows), BF, (width, TILE), column_block),
        ],
        rows // TILE,
        2 * rows * width * width,
        name="project_out",
    )


def feed_up(normed, w_up, bias):
    rows, width = normed.shape
    wide = w_up.shape[1]
    outer = math.sqrt(2 / math.pi)
    cubic = 0.044715

    tile = min(512, wide)

    def kernel(_, ins, outs, weights, scratch):
        value, slope = outs
        columns = pl.ds(pl.multiple_of(pl.program_id(0) * tile, tile), tile)
        u = dot(ins[0][...], weights[0][:, columns]) + ins[1][...]
        square = u * u
        half = 0.5 + 0.5 * jnp.tanh(u * (outer + outer * cubic * square))
        gelu = u * half
        value[...] = gelu.astype(BF)
        rest = gelu * (1.0 - half) * (2 * outer + 6 * outer * cubic * square)
        slope[...] = (half + rest).astype(BF)

    return run(
        kernel,
        [w_up],
        [(normed, (rows, width), fixed_block), (bias, (1, tile), column_block)],
        [((rows, wide), BF, (rows, tile), column_block)] * 2,
        wide // tile,
        2 * rows * width * wide,
        name="feed_up",
        stages=4,
    )


def feed_down(activated, slope, residual, upstream, params, w_down):
    rows, wide = activated.shape
    width = residual.shape[1]

    def kernel(_, ins, outs, weights, scratch):
        act, slope, residual, upstream, params = ins
        mixed, grad_hidden, sum_up, sum_down = outs
        w = weights[0]
        value = residual[...] + dot(act[...], w[...]) + params[7:8]
        mixed[...] = value.astype(BF)
        dy = upstream[...]
        sums = []
        for start in range(0, wide, width):
            columns = slice(start, start + width)
            grad = dot(dy, w[columns, :], NT).astype(BF).astype(F32)
            low = (grad * slope[:, columns].astype(F32)).astype(BF)
            grad_hidden[:, columns] = low
            sums.append(jnp.sum(low.astype(F32), 0, keepdims=True))
        accumulate(sum_up, [jnp.concatenate(sums, axis=1)])
        accumulate(sum_down, [jnp.sum(dy.astype(F32), 0, keepdims=True)])

    return run(
        kernel,
        [w_down],
        [
            (activated, (TILE, wide), row_block),
            (slope, (TILE, wide), row_block),
            (residual, (TILE, width), row_block),
            (upstream, (TILE, width), row_block),
            (params, (16, width), fixed_block),
        ],
        [
            ((rows, width), BF, (TILE, width), row_block),
            ((rows, wide), BF, (TILE, wide), row_block),
            ((8, wide), F32, (8, wide), fixed_block),
            ((8, width), F32, (8, width), fixed_block),
        ],
        rows // TILE,
        4 * rows * width * wide,
        name="feed_down",
        share=LONG,
    )


def feed_back(grad_hidden, residual, upstream, params, w_up, w_o):
    rows, width = residual.shape
    wide = grad_hidden.shape[1]

    def kernel(_, ins, outs, weights, scratch):
        du, residual, upstream, params = ins
        grad_residual, grad_att, grad_context, sums = outs
        grad = dot(du[...], weights[0][...], NT)
        part, gain, shift = normalise_back(grad, residual[...], params[5:6])
        total = upstream[...].astype(F32) + part
        grad_residual[...] = total
        low = total.astype(BF)
        grad_att[...] = low
        grad_context[...] = dot(low, weights[1][...], NT).astype(BF)
        accumulate(sums, [jnp.sum(low.astype(F32), 0, keepdims=True), gain, shift])

    return run(
        kernel,
        [w_up, w_o],
        [
            (grad_hidden, (TILE, wide), row_block),
            (residual, (TILE, width), row_block),
            (upstream, (TILE, width), row_block),
            (params, (16, width), fixed_block),
        ],
        [
            ((rows, width), F32, (TILE, width), row_block),
            ((rows, width), BF, (TILE, width), row_block),
            ((rows, width), BF, (TILE, width), row_block),
            ((8, width), F32, (8, width), fixed_block),
        ],
        rows // TILE,
        2 * rows * width * (wide + width),
        name="feed_back",
        share=LONG,
    )


def project_back(grads, grad_residual, x, params, w_qkv, first, count):
    width = x.shape[1]
    each = width // GROUPS

    def kernel(_, ins, outs, weights, scratch):
        grad_residual, x_ref, params = ins[:3]
        grad_in, sums = outs
        w = weights[0]
        grad = None
        biases = []
        for part in range(3):
            cut = [ref[part] for ref in ins[3:]]
            low = jnp.concatenate(cut, axis=1)
            if part != 1:
                biases.append(jnp.sum(low.astype(F32), 0, keepdims=True))
            value = dot(low, w[:, part * width : (part + 1) * width], NT)
            grad = value if grad is None else grad + value
        part, gain, shift = normalise_back(grad, x_ref[...].astype(F32), params[0:1])
        grad_in[...] = (grad_residual[...] + part).astype(BF)
        accumulate(sums, [gain, shift] + biases)

    return run(
        kernel,
        [w_qkv],
        [
            (grad_residual, (TILE, width), shifted_row_block),
            (x, (TILE, width), shifted_row_block),
            (params, (16, width), fixed_block),
        ]
        + [(g, (3, TILE, each), shifted_part_block) for g in grads],
        [
            ((count * TILE, width), BF, (TILE, width), row_block),
            ((8, width), F32, (8, width), fixed_block),
        ],
        count,
        6 * count * TILE * width * width,
        scalars=[first],
        name="project_back",
    )


def weight_grad(grid, clock, pairs, order):
    if not grid.cube:
        return Summed(jnp.concatenate([dot(turned, part) for turned, right in pairs for part in right], axis=1))
    features, rows = pairs[0][0].shape
    tile = min(512, *(right.shape[2] for _, right in pairs))
    counts = [right.shape[0] * right.shape[2] // tile for _, right in pairs]
    columns = sum(counts) * tile
    shard = features // grid.nz // 8
    places, shape = leading(grid, order)

    def kernel(scalars, ins, outs, weights, scratch):
        first = scalars[0] == 0
        step = pl.program_id(0)

        def work(turned, right, low, high):
            value = dot(turned[...], right[0]).astype(BF)
            for (z, y, x), at in places:
                start = ((z * 2 + y) * 4 + x) * shard
                low[at * shard : (at + 1) * shard] = value[start : start + shard]
                start += 2 * shard
                high[at * shard : (at + 1) * shard] = value[start : start + shard]

        done = 0
        for j, count in enumerate(counts):
            here = (step >= done) & (step < done + count)
            done += count

            @pl.when(here & first)
            def _():
                work(ins[2 * j], ins[2 * j + 1], *outs)

            @pl.when(here & jnp.logical_not(first))
            def _():
                work(ins[2 * j], ins[2 * j + 1], outs[1], outs[0])

    ins, done = [], 0
    for (turned, right), count in zip(pairs, counts):
        per = right.shape[2] // tile

        def block(i, done=done, count=count, per=per):
            j = jnp.clip(i - done, 0, count - 1)
            return (j // per, 0, j % per)

        turned, right = clock(turned, right)
        ins += [(turned, (features, rows), fixed_block), (right, (1, rows, tile), block)]
        done += count
    kept, sent = run(
        kernel,
        [],
        ins,
        [((features // 2, columns), BF, (features // 2, tile), column_block)] * 2,
        sum(counts),
        2 * rows * features * columns,
        scalars=[grid.core],
        name=WG + str(columns),
    )
    shape += (shard, columns)
    kept, sent = clock(kept, sent)
    return Scatter(grid, clock, kept.reshape(shape), sent.reshape(shape), order)


def weight_grad_turned(grid, clock, turned, right, order):
    features, rows = turned.shape
    each = right.shape[1] // (grid.nz * 8)
    places, shape = leading(grid, order)

    def kernel(scalars, ins, outs, weights, scratch):
        first = scalars[0] == 0
        value = dot(ins[0][...], ins[1][...]).astype(BF)

        def store(low, high):
            for (z, y, x), at in places:
                start = ((z * 2 + y) * 4 + x) * each
                low[at] = value[:, start : start + each]
                start += 2 * each
                high[at] = value[:, start : start + each]

        @pl.when(first)
        def _():
            store(*outs)

        @pl.when(jnp.logical_not(first))
        def _():
            store(outs[1], outs[0])

    tile = min(256, features)
    shape += (features, each)
    turned, right = clock(turned, right)
    kept, sent = run(
        kernel,
        [],
        [(turned, (tile, rows), row_block), (right, right.shape, fixed_block)],
        [((grid.nz * 4, features, each), BF, (grid.nz * 4, tile, each), lambda i: (0, i, 0))] * 2,
        features // tile,
        2 * rows * features * right.shape[1],
        scalars=[grid.core],
        name=WG + "turned",
    )
    kept, sent = clock(kept, sent)
    return Scatter(grid, clock, kept.reshape(shape), sent.reshape(shape), order)


def leading(grid, order):
    counts = {"z": grid.nz, "y": 2, "x": 2}
    places = []
    for z in range(grid.nz):
        for y in range(2):
            for x in range(2):
                here = {"z": z, "y": y, "x": x}
                at = 0
                for axis in order:
                    at = at * counts[axis] + here[axis]
                places.append(((z, y, x), at))
    return places, tuple(counts[axis] for axis in order)


def shards(tokens, cotangent, segments, global_blocks, random_blocks, *params):
    grid = Grid()
    gain1, shift1, w_q, b_q, w_k, w_v, b_v, w_o, b_o, gain2, shift2, w_up, b_up, w_down, b_down = params
    count = tokens.shape[0]
    width = tokens.shape[-1]
    wide = w_up.shape[1]
    each = w_v.shape[0]
    devices = grid.dp * grid.group
    replicas = max(1, grid.group // count)

    inputs = to_whole(grid, tokens)
    n, length = inputs.shape[:2]
    rows = n * length
    inputs = inputs.reshape(rows, width)
    vectors = [gain1, shift1, b_q, b_v, b_o, gain2, shift2, b_down]
    extra = jnp.concatenate([*vectors, b_up]).reshape(-1, each).T
    extra = jnp.pad(extra, ((0, 0), (0, 128 - extra.shape[1])))

    clock = Clock()
    first = gather(jnp.concatenate([w_q, w_k], axis=1))
    second = Gather(grid, jnp.concatenate([w_v, w_o, extra], axis=1))
    inputs = second.near(clock, inputs)
    third = Gather(grid, w_up)
    fourth = gather(w_down)
    if grid.group > 1:
        place = lax.axis_index(SEQ)
        start = place * n if count % grid.group == 0 else place % count
        segments, global_blocks, random_blocks = (
            lax.dynamic_slice_in_dim(a, start, n, 0) for a in (segments, global_blocks, random_blocks)
        )
    mask = attention_mask(segments, global_blocks, random_blocks)

    second = second.pieces(clock)
    inputs = third.near(clock, inputs)
    w_qkv = columns_of((first, 0, 2 * width), (second, 0, width))
    w_o, extra = columns_of((second, width, width)), columns_of((second, 2 * width, 128))
    inputs = clock(inputs)
    qkv, normed1_turned, params = clock(*project_in(inputs, w_qkv, extra))
    qkv = qkv.reshape(n, length, 3 * width)
    upstream = to_whole(grid, clock(cotangent)).reshape(rows, width)
    attended = []
    for g in range(GROUPS):
        qkv, mask = clock(qkv, mask)
        attended.append(clock(*attention_forward(qkv, mask, g)))
    contexts = [a[0].reshape(rows, -1) for a in attended]
    w_up, w_down = columns_of((third.pieces(clock), 0, wide)), columns_of((fourth, 0, width))
    contexts[0] = clock(contexts[0])
    residual, normed2, normed2_turned, context_turned = clock(*project_out(contexts, inputs, params, w_o))
    bias_up = params[8 : 8 + wide // width].reshape(-1, devices, each).transpose(1, 0, 2).reshape(1, -1)
    activated, slope = clock(*feed_up(normed2, w_up, bias_up))

    upstream_turned = upstream.T
    if grid.cube:
        sum_w_down = weight_grad_turned(grid, clock, upstream_turned, activated, "yzx")
    else:
        sum_w_down = Summed(dot(activated, upstream, TN))
    activated = clock(activated)
    mixed, grad_hidden, sum_up, sum_down = clock(
        *feed_down(activated, slope, residual, upstream, params, w_down)
    )
    mixed = FromWhole(grid, clock, mixed.reshape(n, length, width), count)
    sum_w_down.step()
    sum_w_up = weight_grad(grid, clock, [(normed2_turned, grad_hidden[None])], "xyz")
    grad_hidden = clock(grad_hidden)
    grad_residual, grad_att, grad_context, sums2 = clock(
        *feed_back(grad_hidden, residual, upstream, params, w_up, w_o)
    )
    sum_w_up.step()
    sum_w_down.step()
    grad_context = grad_context.reshape(n, length, width)
    grads, sums_qkv = [], []
    for g in range(GROUPS):
        grad_context = clock(grad_context)
        grad = clock(attention_backward(qkv, grad_context, *attended[g], g)).reshape(3, rows, -1)
        grads.append(grad)
        if g > 0:
            sum_w_up.step()
            sums_qkv[0].step()
        pairs = [(normed1_turned, grad)] + [(context_turned, grad_att[None])] * (g == 0)
        sums_qkv.append(weight_grad(grid, clock, pairs, "yxz" if g == 0 else "yzx"))
        if g == 0:
            sum_w_down.step()
            sum_w_up.step()
            mixed = mixed.result()
    sums_qkv[1].step()
    steps = rows // TILE
    grads[-1] = clock(grads[-1])
    grad_inputs, sums1 = clock(*project_back(grads, grad_residual, inputs, params, w_qkv, 0, steps))
    sum_w_up.wait(clock)
    sums_qkv[0].step()
    grad_inputs = FromWhole(grid, clock, grad_inputs.reshape(n, length, width), count)
    sums_qkv[1].step(LONG)
    sums_qkv[1].step()
    sums1, sums2, sum_up, sum_down = clock(sums1, sums2, sum_up, sum_down)
    vectors = jnp.concatenate([sums1[:4], sums2[:3], sum_down[:1]])
    vectors = vectors.reshape(8, devices, each).transpose(1, 0, 2).reshape(devices, -1)
    vectors = jnp.concatenate([vectors, sum_up[:1].reshape(devices, -1)], axis=1)
    if grid.cube:
        vectors = halve(vectors.reshape(grid.nz, 2, 2, 2, -1, 128), grid.core, 2, grid.over_core)
    sums_qkv[0].step(LONG)
    if grid.cube:
        vectors = halve(clock(vectors), grid.y, 1, grid.over_y)
        sums_qkv[0].wait(clock)
        vectors = halve(clock(vectors), grid.x, 1, grid.over_x)
    grad_inputs = grad_inputs.result()
    if grid.cube:
        parts = [pick(vectors, (grid.z + k) % grid.nz, 0) for k in range(grid.nz)]
        vectors = total(parts[:1] + [grid.along_z(part, k) for k, part in enumerate(parts) if k])
    else:
        vectors = lax.psum_scatter(vectors, BOTH, scatter_dimension=0, tiled=True)
    vectors = vectors + clock.token[0, 0]

    share = 1.0 / replicas
    grad_w_down = sum_w_down.result() * share
    if grid.cube:
        grad_w_down = grad_w_down.T
    grad_w_up = sum_w_up.result() * share
    ended = [moving.result() * share for moving in sums_qkv]
    cut = width // GROUPS
    grad_w_o = ended[0][:, 3 * cut :]
    grad_w_q, grad_w_k, grad_w_v = (
        jnp.concatenate([e[:, j * cut : (j + 1) * cut] for e in ended], axis=1) for j in range(3)
    )
    vectors = (vectors * share).reshape(-1)
    grad_b_up = vectors[8 * each :]
    grad_gain1, grad_shift1, grad_b_q, grad_b_v, grad_b_o, grad_gain2, grad_shift2, grad_b_down = (
        vectors[j * each : (j + 1) * each] for j in range(8)
    )
    return (
        mixed, grad_inputs, grad_gain1, grad_shift1, grad_w_q, grad_b_q, grad_w_k, grad_w_v, grad_b_v,
        grad_w_o, grad_b_o, grad_gain2, grad_shift2, grad_w_up, grad_b_up, grad_w_down, grad_b_down,
    )


def halve(value, mine, dim, move):
    return pick(value, mine, dim) + move(pick(value, 1 - mine, dim))


def solution(mesh):
    rows = P(DP, SEQ, None)
    vector, matrix = P(BOTH), P(BOTH, None)
    params = (
        vector, vector, matrix, vector, matrix, matrix, vector, matrix, vector, vector, vector, matrix,
        vector, matrix, vector,
    )
    in_specs = (rows, rows, P(DP, None), P(DP, None), P(DP, None, None)) + params
    out_specs = (rows, rows) + params
    return jax.shard_map(shards, mesh=mesh, in_specs=in_specs, out_specs=out_specs, check_vma=False)
```

```python
from functools import partial
import math

import jax
import jax.numpy as jnp
from jax import lax
from jax.experimental import pallas as pl
from jax.experimental.pallas import tpu as pltpu
from jax.sharding import PartitionSpec as P

HEADS = 16
BLK = 64
EPSILON = 1e-06
MASKED = -1e30
DP, SEQ = "dp", "seq"
BOTH = (DP, SEQ)
BF, F32 = jnp.bfloat16, jnp.float32
NT = (((1,), (1,)), ((), ()))
NN = (((1,), (0,)), ((), ()))
TN = (((0,), (0,)), ((), ()))
VMEM_BYTES = 60 * 2**20
TILE = 256
GROUPS = 2
LONG, SHORT = 5.0, 0.05
WG, SUM = "weight_grad_", "sum_"


def cost(flops):
    return pl.CostEstimate(flops=int(flops), bytes_accessed=0, transcendentals=0)


def dot(left, right, dims=NN):
    return lax.dot_general(left, right, dims, preferred_element_type=F32)


class Grid:
    def __init__(self):
        self.dp = lax.axis_size(DP)
        self.group = lax.axis_size(SEQ)
        self.cube = self.group == 2 and self.dp % 4 == 0
        if self.cube:
            self.nz = self.dp // 4
            place = lax.axis_index(DP)
            self.x = lax.axis_index(SEQ)
            self.z, self.y, self.core = place // 4, place // 2 % 2, place % 2

    def over_x(self, v):
        return lax.ppermute(v, SEQ, [(0, 1), (1, 0)])

    def over_y(self, v):
        return lax.ppermute(v, DP, [(i, i ^ 2) for i in range(self.dp)])

    def over_xy(self, v):
        pairs = [(2 * i + x, 2 * (i ^ 2) + 1 - x) for i in range(self.dp) for x in range(2)]
        return lax.ppermute(v, BOTH, pairs)

    def over_core(self, v):
        return lax.ppermute(v, DP, [(i, i ^ 1) for i in range(self.dp)])

    def along_z(self, v, k):
        return lax.ppermute(v, DP, [(i, (i + 4 * k) % self.dp) for i in range(self.dp)])

    def device(self, c, y, x, k):
        z = (self.z - k) % self.nz
        return ((z * 2 + (self.y ^ y)) * 2 + (self.core ^ c)) * 2 + (self.x ^ x)


class Weight:
    def __init__(self, shape):
        self.shape, self.arrays, self.copies, self.rows_at = shape, [], [], []

    def add(self, array, index, rows, row, source=0, width=None, target=0):
        for i, known in enumerate(self.arrays):
            if known is array:
                break
        else:
            i = len(self.arrays)
            self.arrays.append(array)
        self.copies.append((i, index, rows, source, width or array.shape[-1], target))
        self.rows_at.append(row)


def whole_weight(array):
    weight = Weight(array.shape)
    weight.add(array, None, array.shape[0], 0)
    return weight


def columns_of(*parts):
    pieces = parts[0][0]
    weight = Weight((len(pieces) * pieces[0][0].shape[1], sum(width for _, _, width in parts)))
    target = 0
    for pieces, start, width in parts:
        for array, index, device in pieces:
            rows = array.shape[1]
            weight.add(array, index, rows, device * rows, start, width, target)
        target += width
    return weight


def gather(shard):
    every = lax.all_gather(shard, BOTH, axis=0)
    return [(every, i, i) for i in range(every.shape[0])]


class Gather:
    def __init__(self, grid, shard):
        self.grid = grid
        if not grid.cube:
            self.all = gather(shard)
            return
        shard = shard[None]
        self.got = [shard] + [grid.along_z(shard, k) for k in range(1, grid.nz)]

    def near(self, clock, wait):
        if not self.grid.cube:
            return wait
        own = jnp.concatenate(self.got)
        own, wait = clock(own, wait)
        self.got = [own, self.grid.over_xy(own), self.grid.over_x(own), self.grid.over_y(own)]
        return wait

    def pieces(self, clock):
        grid = self.grid
        if not grid.cube:
            return self.all
        self.got = clock(*self.got)
        pieces = []
        for (y, x), piece in zip(((0, 0), (1, 1), (0, 1), (1, 0)), self.got):
            for c, array in enumerate((piece, grid.over_core(piece))):
                pieces += [(array, k, grid.device(c, y, x, k)) for k in range(grid.nz)]
        return pieces


class Clock:
    def __init__(self):
        self.token = None

    def __call__(self, *values):
        if self.token is None:
            self.token = jnp.zeros((8, 128), F32)
        *values, self.token = lax.optimization_barrier((*values, self.token))
        return values[0] if len(values) == 1 else values


def run(kernel, weights, ins, outs, steps, flops, scratch=(), scalars=(), name=None, share=SHORT, stages=1):
    rows_at = [row for w in weights for row in w.rows_at] + list(scalars)
    rows_at = jnp.stack([jnp.asarray(row, jnp.int32) for row in rows_at] or [jnp.int32(0)])
    moves = []
    for which, w in enumerate(weights):
        cut = w.shape[1] // stages
        for n, (i, index, rows, source, width, target) in enumerate(w.copies):
            at = target
            while at < target + width:
                size = min(cut - at % cut, target + width - at)
                moves.append((at // cut, which, n, (i, index, rows, source + at - target, size, at)))
                at += size
    moves.sort(key=lambda move: move[0])
    bases = [sum(len(w.copies) for w in weights[:j]) for j in range(len(weights))]
    n_copies = sum(len(w.copies) for w in weights)
    n_pieces = [len(w.arrays) for w in weights]

    def body(at, *refs):
        refs = list(refs)

        def take(count):
            taken, refs[:count] = refs[:count], []
            return taken

        piece_refs = [take(count) for count in n_pieces]
        in_refs, out_refs = take(len(ins)), take(len(outs))
        held = take(len(weights))
        sems = take(1)[0] if moves else None

        def copies(stage=None):
            for n, (due, which, row, (i, index, rows, source, width, target)) in enumerate(moves):
                if stage is None or due == stage:
                    ref = piece_refs[which][i] if index is None else piece_refs[which][i].at[index]
                    yield pltpu.make_async_copy(
                        ref.at[:, pl.ds(source, width)],
                        held[which].at[pl.ds(pl.multiple_of(at[bases[which] + row], rows), rows), pl.ds(target, width)],
                        sems.at[n],
                    )

        step = pl.program_id(0)
        if moves:

            @pl.when(step == 0)
            def _():
                for copy in copies():
                    copy.start()

            for stage in range(stages):

                @pl.when(step == stage * (steps // stages))
                def _():
                    for copy in copies(stage):
                        copy.wait()

        values = [at[n_copies + i] for i in range(len(scalars))]
        kernel(values, in_refs, out_refs, held, refs)

    anywhere = pl.BlockSpec(memory_space=pl.ANY)

    def spec(block, index):
        if index is shifted_row_block:
            return pl.BlockSpec(block, lambda i, at: (at[n_copies] + i, 0))
        if index is shifted_part_block:
            return pl.BlockSpec(block, lambda i, at: (0, at[n_copies] + i, 0))
        return pl.BlockSpec(block, lambda i, at: index(i))

    semaphores = [pltpu.SemaphoreType.DMA((len(moves),))] if moves else []
    return pl.pallas_call(
        body,
        grid_spec=pltpu.PrefetchScalarGridSpec(
            num_scalar_prefetch=1,
            grid=(steps,),
            in_specs=[anywhere] * sum(n_pieces) + [spec(block, index) for _, block, index in ins],
            out_specs=[spec(block, index) for _, _, block, index in outs],
            scratch_shapes=[pltpu.VMEM(w.shape, BF) for w in weights] + semaphores + list(scratch),
        ),
        out_shape=[jax.ShapeDtypeStruct(shape, dtype) for shape, dtype, _, _ in outs],
        compiler_params=pltpu.CompilerParams(vmem_limit_bytes=VMEM_BYTES),
        name=name,
        cost_estimate=cost(flops * share),
    )(rows_at, *[a for w in weights for a in w.arrays], *[a for a, _, _ in ins])


def pick(array, index, axis):
    return lax.dynamic_index_in_dim(array, index, axis, keepdims=False)


def total(terms):
    value = terms[0].astype(F32)
    for term in terms[1:]:
        value = value + term.astype(F32)
    return value


def split_sum(terms, order, name, share):
    parts, size = terms[0].shape[0], terms[0].size
    rest = terms[0].shape[1:]
    columns = terms[0].shape[-1]
    rows = size // parts // columns
    tile = rows
    while tile * columns > 2**18 and tile % 32 == 0:
        tile //= 2
    flat = [t.reshape(parts, rows, columns) for t in terms]
    wanted = len(order)

    def kernel(at, *refs):
        del at
        for j in range(wanted):
            value = refs[j][0].astype(F32)
            for i in range(1, len(terms)):
                value = value + refs[i * wanted + j][0].astype(F32)
            refs[len(terms) * wanted + j][...] = value.astype(terms[0].dtype)

    outs = pl.pallas_call(
        kernel,
        grid_spec=pltpu.PrefetchScalarGridSpec(
            num_scalar_prefetch=1,
            grid=(rows // tile,),
            in_specs=[
                pl.BlockSpec((1, tile, columns), lambda i, at, j=j: (at[j], i, 0))
                for _ in terms
                for j in range(wanted)
            ],
            out_specs=[pl.BlockSpec((tile, columns), lambda i, at: (i, 0))] * wanted,
        ),
        out_shape=[jax.ShapeDtypeStruct((rows, columns), terms[0].dtype)] * wanted,
        compiler_params=pltpu.CompilerParams(vmem_limit_bytes=VMEM_BYTES),
        name=name,
        cost_estimate=cost(2e10 * share),
    )(jnp.stack(order).astype(jnp.int32), *[t for t in flat for _ in range(wanted)])
    return [out.reshape(rest) for out in outs]


class Scatter:
    def __init__(self, grid, clock, kept, sent, order):
        self.grid, self.clock, self.order = grid, clock, order
        self.own, self.got = [kept], [grid.over_core(sent)]

    def step(self, share=SHORT):
        grid, axis, self.order = self.grid, self.order[0], self.order[1:]
        terms = self.clock(*self.own, *self.got)
        if axis == "z":
            places = [(grid.z + k) % grid.nz for k in range(grid.nz)]
            own, *parts = self.clock(*split_sum(terms, places, SUM + axis, share))
            self.got = [grid.along_z(part, k) for k, part in enumerate(parts, 1)]
        else:
            mine, move = (grid.y, grid.over_y) if axis == "y" else (grid.x, grid.over_x)
            own, part = self.clock(*split_sum(terms, [mine, 1 - mine], SUM + axis, share))
            self.got = [move(part)]
        self.own = [own]

    def wait(self, clock):
        if self.got:
            self.got = list(clock(*self.got))

    def result(self):
        return total(self.own + self.got)


class Summed:
    def __init__(self, value):
        self.value, self.own = value, []

    def step(self, share=SHORT):
        pass

    def wait(self, clock):
        pass

    def result(self):
        return lax.psum_scatter(self.value, BOTH, scatter_dimension=0, tiled=True)


def to_whole(grid, part):
    group, count = grid.group, part.shape[0]
    if group == 1:
        return part
    place = lax.axis_index(SEQ)
    if group == 2 and count == 2:
        kept, got = pick(part, place, 0), grid.over_x(pick(part, 1 - place, 0))
        first = jnp.where(place == 0, kept, got)
        second = jnp.where(place == 0, got, kept)
        return jnp.concatenate([first, second])[None]
    if count % group == 0:
        return lax.all_to_all(part, SEQ, split_axis=0, concat_axis=1, tiled=True)
    every = lax.all_gather(part, SEQ, axis=1, tiled=True)
    return pick(every, place % count, 0)[None]


class FromWhole:
    def __init__(self, grid, clock, whole, count):
        self.grid, self.clock, self.whole, self.count = grid, clock, whole, count
        self.swap = grid.group == 2 and count == 2
        if self.swap:
            place = lax.axis_index(SEQ)
            halves = whole.reshape(2, -1, whole.shape[-1])
            self.kept, self.got = pick(halves, place, 0), grid.over_x(pick(halves, 1 - place, 0))

    def result(self):
        group, whole, count = self.grid.group, self.whole, self.count
        place = lax.axis_index(SEQ)
        if self.swap:
            got = self.clock(self.got)
            return jnp.stack([jnp.where(place == 0, self.kept, got), jnp.where(place == 0, got, self.kept)])
        if group == 1:
            return whole
        if count % group == 0:
            return lax.all_to_all(whole, SEQ, split_axis=1, concat_axis=0, tiled=True)
        every = lax.all_gather(whole[0], SEQ, axis=0)[:count]
        rows = whole.shape[1] // group
        return lax.dynamic_slice_in_dim(every, place * rows, rows, 1)


def attention_forward_kernel(
    q_ref, k_ref, v_ref, mask_ref, out_ref, total_ref, weight_ref, *, head, chunk
):
    factor = head**-0.5 * math.log2(math.e)
    rows = q_ref.shape[1]
    for h in range(q_ref.shape[2] // head):
        lanes = slice(h * head, (h + 1) * head)
        keys, values = k_ref[0, :, lanes], v_ref[0, :, lanes]
        for start in range(0, rows, chunk):
            part = slice(start, start + chunk)
            scores = dot(keys, q_ref[0, part, lanes], NT)
            weights = jnp.exp2(scores * factor + mask_ref[0, :, part])
            total = jnp.sum(weights, axis=0, keepdims=True)
            low = weights.astype(BF)
            weight_ref[0, 0, h, :, part] = low
            summed = dot(values, low, TN)
            total_ref[0, 0, h : h + 1, part] = total
            out_ref[0, part, lanes] = (summed / total).T.astype(BF)


def attention_backward_kernel(
    q_ref, k_ref, v_ref, weight_ref, grad_ref, ctx_ref, total_ref, out_ref, dk_sum, dv_sum, *, head, chunk
):
    scale = head**-0.5
    rows = q_ref.shape[1]
    for h in range(q_ref.shape[2] // head):
        lanes = slice(h * head, (h + 1) * head)
        keys, values = k_ref[0, :, lanes], v_ref[0, :, lanes]
        keys_t = keys.T
        for start in range(0, rows, chunk):
            part = slice(start, start + chunk)
            queries = q_ref[0, part, lanes]
            low = weight_ref[0, 0, h, :, part]
            inverse = 1.0 / total_ref[0, 0, h : h + 1, part]
            grad = grad_ref[0, part, lanes].astype(F32)
            product = (grad * ctx_ref[0, part, lanes].astype(F32)).T
            grad_total = -jnp.sum(product, axis=0, keepdims=True) * inverse
            grad_summed = (grad.T * inverse).astype(BF)
            grad_probs = dot(values, grad_summed)
            grad_scores = (low.astype(F32) * (grad_probs + grad_total)).astype(BF)
            dv_part = dot(low, grad_summed, NT)
            dk_part = dot(grad_scores, queries)
            if start == 0:
                dv_sum[...] = dv_part
                dk_sum[...] = dk_part
            else:
                dv_sum[...] += dv_part
                dk_sum[...] += dk_part
            out_ref[0, 0, part, lanes] = (dot(keys_t, grad_scores).T * scale).astype(BF)
        out_ref[1, 0, :, lanes] = (dk_sum[...] * scale).astype(BF)
        out_ref[2, 0, :, lanes] = dv_sum[...].astype(BF)


def attention_specs(length, width, group):
    head = width // HEADS
    lanes = max(128, head)
    steps = width // lanes // GROUPS

    def columns(which):
        return pl.BlockSpec((1, length, lanes), lambda b, p: (b, 0, (which * GROUPS + group) * steps + p))

    own = pl.BlockSpec((1, length, lanes), lambda b, p: (b, 0, p))
    mask = pl.BlockSpec((1, length, length), lambda b, p: (b, 0, 0))
    totals = pl.BlockSpec((1, 1, lanes // head, length), lambda b, p: (b, p, 0, 0))
    weights = pl.BlockSpec((1, 1, lanes // head, length, length), lambda b, p: (b, p, 0, 0, 0))
    return head, lanes, steps, columns, own, mask, totals, weights


def attention_forward(qkv, mask, group):
    count, length, width = qkv.shape
    width = width // 3
    head, lanes, steps, columns, own, mask_spec, totals, weights = attention_specs(length, width, group)
    return pl.pallas_call(
        partial(attention_forward_kernel, head=head, chunk=512),
        grid=(count, steps),
        in_specs=[columns(0), columns(1), columns(2), mask_spec],
        out_specs=[own, totals, weights],
        out_shape=[
            jax.ShapeDtypeStruct((count, length, width // GROUPS), BF),
            jax.ShapeDtypeStruct((count, steps, lanes // head, length), F32),
            jax.ShapeDtypeStruct((count, steps, lanes // head, length, length), BF),
        ],
        name="attention_forward",
        compiler_params=pltpu.CompilerParams(vmem_limit_bytes=VMEM_BYTES),
        cost_estimate=cost(12 * count * length * length * width // GROUPS),
    )(qkv, qkv, qkv, mask)


def attention_backward(qkv, grad, context, totals_in, weights_in, group):
    count, length, width = grad.shape
    head, lanes, steps, columns, own, mask_spec, totals, weights = attention_specs(length, width, group)
    grads = pl.BlockSpec((3, 1, length, lanes), lambda b, p: (0, b, 0, p))
    return pl.pallas_call(
        partial(attention_backward_kernel, head=head, chunk=256),
        grid=(count, steps),
        in_specs=[columns(0), columns(1), columns(2), weights, columns(0), own, totals],
        out_specs=grads,
        out_shape=jax.ShapeDtypeStruct((3, count, length, width // GROUPS), BF),
        scratch_shapes=[pltpu.VMEM((length, head), F32)] * 2,
        name="attention_backward",
        compiler_params=pltpu.CompilerParams(vmem_limit_bytes=VMEM_BYTES),
        cost_estimate=cost(26 * count * length * length * width * (LONG if group else SHORT)),
    )(qkv, qkv, qkv, weights_in, grad, context, totals_in)


def attention_mask(segments, globals_pair, randoms):
    count, blocks = randoms.shape[:2]
    length = segments.shape[1]
    numbers = jnp.arange(blocks, dtype=jnp.int32)
    chosen = jnp.any(globals_pair[:, :, None] == numbers, axis=1)
    nearby = jnp.abs(numbers[:, None] - numbers[None, :]) <= 1
    picked = jnp.any(randoms[:, :, :, None] == numbers, axis=2)
    seen = chosen[:, :, None] | chosen[:, None, :] | nearby[None] | picked
    seen = jnp.swapaxes(seen, 1, 2)[:, :, None, :, None]
    seen = jnp.broadcast_to(seen, (count, blocks, BLK, blocks, BLK)).reshape(count, length, length)
    same = segments[:, :, None] == segments[:, None, :]
    return jnp.where(seen & same, 0.0, MASKED).astype(F32)


def normalise(values):
    centred = values - jnp.mean(values, -1, keepdims=True)
    inverse = lax.rsqrt(jnp.mean(centred * centred, -1, keepdims=True) + EPSILON)
    return centred * inverse, inverse


def normalise_back(grad, values, gain):
    unit, inverse = normalise(values)
    inner = grad * gain
    grad_in = inverse * (
        inner - jnp.mean(inner, -1, keepdims=True) - unit * jnp.mean(inner * unit, -1, keepdims=True)
    )
    return grad_in, jnp.sum(grad * unit, 0, keepdims=True), jnp.sum(grad, 0, keepdims=True)


def accumulate(ref, rows):
    first = pl.program_id(0) == 0
    for j, row in enumerate(rows):

        @pl.when(first)
        def _():
            ref[j : j + 1] = row

        @pl.when(jnp.logical_not(first))
        def _():
            ref[j : j + 1] += row


def row_block(i):
    return (i, 0)


def shifted_row_block(i):
    raise NotImplementedError


def shifted_part_block(i):
    raise NotImplementedError


def fixed_block(i):
    return (0, 0)


def column_block(i):
    return (0, i)


def project_in(x, w_qkv, extra):
    rows, width = x.shape

    def kernel(_, ins, outs, weights, scratch):
        qkv, turned, params = outs
        w, small = weights

        @pl.when(pl.program_id(0) == 0)
        def _():
            params[...] = small[...].astype(F32).T[:16]

        unit, _ = normalise(ins[0][...].astype(F32))
        normed = (unit * params[0:1] + params[1:2]).astype(BF)
        turned[...] = normed.T
        for part, bias in enumerate((params[2:3], None, params[3:4])):
            columns = slice(part * width, (part + 1) * width)
            value = dot(normed, w[:, columns])
            qkv[:, columns] = (value if bias is None else value + bias).astype(BF)

    return run(
        kernel,
        [w_qkv, extra],
        [(x, (TILE, width), row_block)],
        [
            ((rows, 3 * width), BF, (TILE, 3 * width), row_block),
            ((width, rows), BF, (width, TILE), column_block),
            ((16, width), F32, (16, width), fixed_block),
        ],
        rows // TILE,
        6 * rows * width * width,
        name="project_in",
    )


def project_out(contexts, x, params, w_o):
    rows, width = x.shape

    def kernel(_, ins, outs, weights, scratch):
        x_ref, params = ins[:2]
        residual, normed, turned, context_turned = outs
        parts = [ref[...] for ref in ins[2:]]
        context = jnp.concatenate(parts, axis=1)
        context_turned[...] = context.T
        value = x_ref[...].astype(F32) + dot(context, weights[0][...]) + params[4:5]
        residual[...] = value
        unit, _ = normalise(value)
        low = (unit * params[5:6] + params[6:7]).astype(BF)
        normed[...] = low
        turned[...] = low.T

    return run(
        kernel,
        [w_o],
        [(x, (TILE, width), row_block), (params, (16, width), fixed_block)]
        + [(c, (TILE, c.shape[1]), row_block) for c in contexts],
        [
            ((rows, width), F32, (TILE, width), row_block),
            ((rows, width), BF, (TILE, width), row_block),
            ((width, rows), BF, (width, TILE), column_block),
            ((width, rows), BF, (width, TILE), column_block),
        ],
        rows // TILE,
        2 * rows * width * width,
        name="project_out",
    )


def feed_up(normed, w_up, bias):
    rows, width = normed.shape
    wide = w_up.shape[1]
    outer = math.sqrt(2 / math.pi)
    cubic = 0.044715

    tile = min(512, wide)

    def kernel(_, ins, outs, weights, scratch):
        value, slope = outs
        columns = pl.ds(pl.multiple_of(pl.program_id(0) * tile, tile), tile)
        u = dot(ins[0][...], weights[0][:, columns]) + ins[1][...]
        square = u * u
        half = 0.5 + 0.5 * jnp.tanh(u * (outer + outer * cubic * square))
        gelu = u * half
        value[...] = gelu.astype(BF)
        rest = gelu * (1.0 - half) * (2 * outer + 6 * outer * cubic * square)
        slope[...] = (half + rest).astype(BF)

    return run(
        kernel,
        [w_up],
        [(normed, (rows, width), fixed_block), (bias, (1, tile), column_block)],
        [((rows, wide), BF, (rows, tile), column_block)] * 2,
        wide // tile,
        2 * rows * width * wide,
        name="feed_up",
        stages=4,
    )


def feed_down(activated, slope, residual, upstream, params, w_down):
    rows, wide = activated.shape
    width = residual.shape[1]

    def kernel(_, ins, outs, weights, scratch):
        act, slope, residual, upstream, params = ins
        mixed, grad_hidden, sum_up, sum_down = outs
        w = weights[0]
        value = residual[...] + dot(act[...], w[...]) + params[7:8]
        mixed[...] = value.astype(BF)
        dy = upstream[...]
        sums = []
        for start in range(0, wide, width):
            columns = slice(start, start + width)
            grad = dot(dy, w[columns, :], NT).astype(BF).astype(F32)
            low = (grad * slope[:, columns].astype(F32)).astype(BF)
            grad_hidden[:, columns] = low
            sums.append(jnp.sum(low.astype(F32), 0, keepdims=True))
        accumulate(sum_up, [jnp.concatenate(sums, axis=1)])
        accumulate(sum_down, [jnp.sum(dy.astype(F32), 0, keepdims=True)])

    return run(
        kernel,
        [w_down],
        [
            (activated, (TILE, wide), row_block),
            (slope, (TILE, wide), row_block),
            (residual, (TILE, width), row_block),
            (upstream, (TILE, width), row_block),
            (params, (16, width), fixed_block),
        ],
        [
            ((rows, width), BF, (TILE, width), row_block),
            ((rows, wide), BF, (TILE, wide), row_block),
            ((8, wide), F32, (8, wide), fixed_block),
            ((8, width), F32, (8, width), fixed_block),
        ],
        rows // TILE,
        4 * rows * width * wide,
        name="feed_down",
        share=LONG,
    )


def feed_back(grad_hidden, residual, upstream, params, w_up, w_o):
    rows, width = residual.shape
    wide = grad_hidden.shape[1]

    def kernel(_, ins, outs, weights, scratch):
        du, residual, upstream, params = ins
        grad_residual, grad_att, grad_context, sums = outs
        grad = dot(du[...], weights[0][...], NT)
        part, gain, shift = normalise_back(grad, residual[...], params[5:6])
        total = upstream[...].astype(F32) + part
        grad_residual[...] = total
        low = total.astype(BF)
        grad_att[...] = low
        grad_context[...] = dot(low, weights[1][...], NT).astype(BF)
        accumulate(sums, [jnp.sum(low.astype(F32), 0, keepdims=True), gain, shift])

    return run(
        kernel,
        [w_up, w_o],
        [
            (grad_hidden, (TILE, wide), row_block),
            (residual, (TILE, width), row_block),
            (upstream, (TILE, width), row_block),
            (params, (16, width), fixed_block),
        ],
        [
            ((rows, width), F32, (TILE, width), row_block),
            ((rows, width), BF, (TILE, width), row_block),
            ((rows, width), BF, (TILE, width), row_block),
            ((8, width), F32, (8, width), fixed_block),
        ],
        rows // TILE,
        2 * rows * width * (wide + width),
        name="feed_back",
        share=LONG,
    )


def project_back(grads, grad_residual, x, params, w_qkv, first, count):
    width = x.shape[1]
    each = width // GROUPS

    def kernel(_, ins, outs, weights, scratch):
        grad_residual, x_ref, params = ins[:3]
        grad_in, sums = outs
        w = weights[0]
        grad = None
        biases = []
        for part in range(3):
            cut = [ref[part] for ref in ins[3:]]
            low = jnp.concatenate(cut, axis=1)
            if part != 1:
                biases.append(jnp.sum(low.astype(F32), 0, keepdims=True))
            value = dot(low, w[:, part * width : (part + 1) * width], NT)
            grad = value if grad is None else grad + value
        part, gain, shift = normalise_back(grad, x_ref[...].astype(F32), params[0:1])
        grad_in[...] = (grad_residual[...] + part).astype(BF)
        accumulate(sums, [gain, shift] + biases)

    return run(
        kernel,
        [w_qkv],
        [
            (grad_residual, (TILE, width), shifted_row_block),
            (x, (TILE, width), shifted_row_block),
            (params, (16, width), fixed_block),
        ]
        + [(g, (3, TILE, each), shifted_part_block) for g in grads],
        [
            ((count * TILE, width), BF, (TILE, width), row_block),
            ((8, width), F32, (8, width), fixed_block),
        ],
        count,
        6 * count * TILE * width * width,
        scalars=[first],
        name="project_back",
    )


def weight_grad(grid, clock, pairs, order):
    if not grid.cube:
        return Summed(jnp.concatenate([dot(turned, part) for turned, right in pairs for part in right], axis=1))
    features, rows = pairs[0][0].shape
    tile = min(512, *(right.shape[2] for _, right in pairs))
    counts = [right.shape[0] * right.shape[2] // tile for _, right in pairs]
    columns = sum(counts) * tile
    shard = features // grid.nz // 8
    places, shape = leading(grid, order)

    def kernel(scalars, ins, outs, weights, scratch):
        first = scalars[0] == 0
        step = pl.program_id(0)

        def work(turned, right, low, high):
            value = dot(turned[...], right[0]).astype(BF)
            for (z, y, x), at in places:
                start = ((z * 2 + y) * 4 + x) * shard
                low[at * shard : (at + 1) * shard] = value[start : start + shard]
                start += 2 * shard
                high[at * shard : (at + 1) * shard] = value[start : start + shard]

        done = 0
        for j, count in enumerate(counts):
            here = (step >= done) & (step < done + count)
            done += count

            @pl.when(here & first)
            def _():
                work(ins[2 * j], ins[2 * j + 1], *outs)

            @pl.when(here & jnp.logical_not(first))
            def _():
                work(ins[2 * j], ins[2 * j + 1], outs[1], outs[0])

    ins, done = [], 0
    for (turned, right), count in zip(pairs, counts):
        per = right.shape[2] // tile

        def block(i, done=done, count=count, per=per):
            j = jnp.clip(i - done, 0, count - 1)
            return (j // per, 0, j % per)

        turned, right = clock(turned, right)
        ins += [(turned, (features, rows), fixed_block), (right, (1, rows, tile), block)]
        done += count
    kept, sent = run(
        kernel,
        [],
        ins,
        [((features // 2, columns), BF, (features // 2, tile), column_block)] * 2,
        sum(counts),
        2 * rows * features * columns,
        scalars=[grid.core],
        name=WG + str(columns),
    )
    shape += (shard, columns)
    kept, sent = clock(kept, sent)
    return Scatter(grid, clock, kept.reshape(shape), sent.reshape(shape), order)


def weight_grad_turned(grid, clock, left, right, order):
    rows, features = left.shape
    each = right.shape[1] // (grid.nz * 8)
    places, shape = leading(grid, order)

    def kernel(scalars, ins, outs, weights, scratch):
        first = scalars[0] == 0
        value = dot(ins[0][...], ins[1][...], TN).astype(BF)

        def store(low, high):
            for (z, y, x), at in places:
                start = ((z * 2 + y) * 4 + x) * each
                low[at] = value[:, start : start + each]
                start += 2 * each
                high[at] = value[:, start : start + each]

        @pl.when(first)
        def _():
            store(*outs)

        @pl.when(jnp.logical_not(first))
        def _():
            store(outs[1], outs[0])

    tile = min(256, features)
    shape += (features, each)
    left, right = clock(left, right)
    kept, sent = run(
        kernel,
        [],
        [(left, (rows, tile), column_block), (right, right.shape, fixed_block)],
        [((grid.nz * 4, features, each), BF, (grid.nz * 4, tile, each), lambda i: (0, i, 0))] * 2,
        features // tile,
        2 * rows * features * right.shape[1],
        scalars=[grid.core],
        name=WG + "turned",
    )
    kept, sent = clock(kept, sent)
    return Scatter(grid, clock, kept.reshape(shape), sent.reshape(shape), order)


def leading(grid, order):
    counts = {"z": grid.nz, "y": 2, "x": 2}
    places = []
    for z in range(grid.nz):
        for y in range(2):
            for x in range(2):
                here = {"z": z, "y": y, "x": x}
                at = 0
                for axis in order:
                    at = at * counts[axis] + here[axis]
                places.append(((z, y, x), at))
    return places, tuple(counts[axis] for axis in order)


def shards(tokens, cotangent, segments, global_blocks, random_blocks, *params):
    grid = Grid()
    gain1, shift1, w_q, b_q, w_k, w_v, b_v, w_o, b_o, gain2, shift2, w_up, b_up, w_down, b_down = params
    count = tokens.shape[0]
    width = tokens.shape[-1]
    wide = w_up.shape[1]
    each = w_v.shape[0]
    devices = grid.dp * grid.group
    replicas = max(1, grid.group // count)

    inputs = to_whole(grid, tokens)
    n, length = inputs.shape[:2]
    rows = n * length
    inputs = inputs.reshape(rows, width)
    vectors = [gain1, shift1, b_q, b_v, b_o, gain2, shift2, b_down]
    extra = jnp.concatenate([*vectors, b_up]).reshape(-1, each).T
    extra = jnp.pad(extra, ((0, 0), (0, 128 - extra.shape[1])))

    clock = Clock()
    first = gather(jnp.concatenate([w_q, w_k], axis=1))
    second = Gather(grid, jnp.concatenate([w_v, w_o, extra], axis=1))
    inputs = second.near(clock, inputs)
    third = Gather(grid, w_up)
    fourth = gather(w_down)
    if grid.group > 1:
        place = lax.axis_index(SEQ)
        start = place * n if count % grid.group == 0 else place % count
        segments, global_blocks, random_blocks = (
            lax.dynamic_slice_in_dim(a, start, n, 0) for a in (segments, global_blocks, random_blocks)
        )
    mask = attention_mask(segments, global_blocks, random_blocks)

    second = second.pieces(clock)
    inputs = third.near(clock, inputs)
    w_qkv = columns_of((first, 0, 2 * width), (second, 0, width))
    w_o, extra = columns_of((second, width, width)), columns_of((second, 2 * width, 128))
    inputs = clock(inputs)
    qkv, normed1_turned, params = clock(*project_in(inputs, w_qkv, extra))
    qkv = qkv.reshape(n, length, 3 * width)
    upstream = to_whole(grid, clock(cotangent)).reshape(rows, width)
    attended = []
    for g in range(GROUPS):
        qkv, mask = clock(qkv, mask)
        attended.append(clock(*attention_forward(qkv, mask, g)))
    contexts = [a[0].reshape(rows, -1) for a in attended]
    contexts[0] = clock(contexts[0])
    residual, normed2, normed2_turned, context_turned = clock(*project_out(contexts, inputs, params, w_o))
    w_up, w_down = columns_of((third.pieces(clock), 0, wide)), columns_of((fourth, 0, width))
    normed2 = clock(normed2)
    bias_up = params[8 : 8 + wide // width].reshape(-1, devices, each).transpose(1, 0, 2).reshape(1, -1)
    activated, slope = clock(*feed_up(normed2, w_up, bias_up))

    if grid.cube:
        sum_w_down = weight_grad_turned(grid, clock, upstream, activated, "yzx")
    else:
        sum_w_down = Summed(dot(activated, upstream, TN))
    activated = clock(activated)
    mixed, grad_hidden, sum_up, sum_down = clock(
        *feed_down(activated, slope, residual, upstream, params, w_down)
    )
    mixed = FromWhole(grid, clock, mixed.reshape(n, length, width), count)
    sum_w_down.step()
    sum_w_up = weight_grad(grid, clock, [(normed2_turned, grad_hidden[None])], "xyz")
    grad_hidden = clock(grad_hidden)
    grad_residual, grad_att, grad_context, sums2 = clock(
        *feed_back(grad_hidden, residual, upstream, params, w_up, w_o)
    )
    mixed = mixed.result()
    sum_w_up.step()
    sum_w_down.step()
    grad_context = grad_context.reshape(n, length, width)
    grads, sums_qkv = [], []
    for g in range(GROUPS):
        grad_context = clock(grad_context)
        grad = clock(attention_backward(qkv, grad_context, *attended[g], g)).reshape(3, rows, -1)
        grads.append(grad)
        if g > 0:
            sum_w_up.step()
            sums_qkv[0].step()
        pairs = [(normed1_turned, grad)] + [(context_turned, grad_att[None])] * (g == 0)
        sums_qkv.append(weight_grad(grid, clock, pairs, "yxz"))
        if g == 0:
            sum_w_down.step()
            sum_w_up.step()
    sums_qkv[1].step()
    steps = rows // TILE
    grads[-1] = clock(grads[-1])
    grad_inputs, sums1 = clock(*project_back(grads, grad_residual, inputs, params, w_qkv, 0, steps))
    sum_w_up.wait(clock)
    sums_qkv[0].step()
    sums_qkv[1].step()
    grad_inputs = clock(grad_inputs)
    grad_inputs = FromWhole(grid, clock, grad_inputs.reshape(n, length, width), count)
    vectors = jnp.concatenate([sums1[:4], sums2[:3], sum_down[:1]])
    vectors = vectors.reshape(8, devices, each).transpose(1, 0, 2).reshape(devices, -1)
    vectors = jnp.concatenate([vectors, sum_up[:1].reshape(devices, -1)], axis=1)
    if grid.cube:
        vectors = halve(clock(vectors).reshape(grid.nz, 2, 2, 2, -1, 128), grid.core, 2, grid.over_core)
    sums_qkv[1].step(LONG)
    sums_qkv[0].step()
    if grid.cube:
        vectors = halve(clock(vectors), grid.y, 1, grid.over_y)
    grad_inputs = grad_inputs.result()
    if grid.cube:
        sums_qkv[1].wait(clock)
        vectors = halve(clock(vectors), grid.x, 1, grid.over_x)
        sums_qkv[0].wait(clock)
        parts = [pick(vectors, (grid.z + k) % grid.nz, 0) for k in range(grid.nz)]
        vectors = total(parts[:1] + [grid.along_z(part, k) for k, part in enumerate(parts) if k])
    else:
        vectors = lax.psum_scatter(vectors, BOTH, scatter_dimension=0, tiled=True)
    vectors = vectors + clock.token[0, 0]

    share = 1.0 / replicas
    grad_w_down = sum_w_down.result() * share
    if grid.cube:
        grad_w_down = grad_w_down.T
    grad_w_up = sum_w_up.result() * share
    ended = [moving.result() * share for moving in sums_qkv]
    cut = width // GROUPS
    grad_w_o = ended[0][:, 3 * cut :]
    grad_w_q, grad_w_k, grad_w_v = (
        jnp.concatenate([e[:, j * cut : (j + 1) * cut] for e in ended], axis=1) for j in range(3)
    )
    vectors = (vectors * share).reshape(-1)
    grad_b_up = vectors[8 * each :]
    grad_gain1, grad_shift1, grad_b_q, grad_b_v, grad_b_o, grad_gain2, grad_shift2, grad_b_down = (
        vectors[j * each : (j + 1) * each] for j in range(8)
    )
    return (
        mixed, grad_inputs, grad_gain1, grad_shift1, grad_w_q, grad_b_q, grad_w_k, grad_w_v, grad_b_v,
        grad_w_o, grad_b_o, grad_gain2, grad_shift2, grad_w_up, grad_b_up, grad_w_down, grad_b_down,
    )


def halve(value, mine, dim, move):
    return pick(value, mine, dim) + move(pick(value, 1 - mine, dim))


def solution(mesh):
    rows = P(DP, SEQ, None)
    vector, matrix = P(BOTH), P(BOTH, None)
    params = (
        vector, vector, matrix, vector, matrix, matrix, vector, matrix, vector, vector, vector, matrix,
        vector, matrix, vector,
    )
    in_specs = (rows, rows, P(DP, None), P(DP, None), P(DP, None, None)) + params
    out_specs = (rows, rows) + params
    return jax.shard_map(shards, mesh=mesh, in_specs=in_specs, out_specs=out_specs, check_vma=False)
```

```python
from functools import partial
import math

import jax
import jax.numpy as jnp
from jax import lax
from jax.experimental import pallas as pl
from jax.experimental.pallas import tpu as pltpu
from jax.sharding import PartitionSpec as P

HEADS = 16
BLK = 64
EPSILON = 1e-06
MASKED = -1e30
DP, SEQ = "dp", "seq"
BOTH = (DP, SEQ)
BF, F32 = jnp.bfloat16, jnp.float32
NT = (((1,), (1,)), ((), ()))
NN = (((1,), (0,)), ((), ()))
TN = (((0,), (0,)), ((), ()))
VMEM_BYTES = 60 * 2**20
TILE = 256
GROUPS = 2
LONG, SHORT = 5.0, 0.05
WG, SUM = "weight_grad_", "sum_"


def cost(flops):
    return pl.CostEstimate(flops=int(flops), bytes_accessed=0, transcendentals=0)


def dot(left, right, dims=NN):
    return lax.dot_general(left, right, dims, preferred_element_type=F32)


class Grid:
    def __init__(self):
        self.dp = lax.axis_size(DP)
        self.group = lax.axis_size(SEQ)
        self.cube = self.group == 2 and self.dp % 4 == 0
        if self.cube:
            self.nz = self.dp // 4
            place = lax.axis_index(DP)
            self.x = lax.axis_index(SEQ)
            self.z, self.y, self.core = place // 4, place // 2 % 2, place % 2

    def over_x(self, v):
        return lax.ppermute(v, SEQ, [(0, 1), (1, 0)])

    def over_y(self, v):
        return lax.ppermute(v, DP, [(i, i ^ 2) for i in range(self.dp)])

    def over_xy(self, v):
        pairs = [(2 * i + x, 2 * (i ^ 2) + 1 - x) for i in range(self.dp) for x in range(2)]
        return lax.ppermute(v, BOTH, pairs)

    def over_core(self, v):
        return lax.ppermute(v, DP, [(i, i ^ 1) for i in range(self.dp)])

    def along_z(self, v, k):
        return lax.ppermute(v, DP, [(i, (i + 4 * k) % self.dp) for i in range(self.dp)])

    def device(self, c, y, x, k):
        z = (self.z - k) % self.nz
        return ((z * 2 + (self.y ^ y)) * 2 + (self.core ^ c)) * 2 + (self.x ^ x)


class Weight:
    def __init__(self, shape):
        self.shape, self.arrays, self.copies, self.rows_at = shape, [], [], []

    def add(self, array, index, rows, row, source=0, width=None, target=0):
        for i, known in enumerate(self.arrays):
            if known is array:
                break
        else:
            i = len(self.arrays)
            self.arrays.append(array)
        self.copies.append((i, index, rows, source, width or array.shape[-1], target))
        self.rows_at.append(row)


def whole_weight(array):
    weight = Weight(array.shape)
    weight.add(array, None, array.shape[0], 0)
    return weight


def columns_of(*parts):
    pieces = parts[0][0]
    weight = Weight((len(pieces) * pieces[0][0].shape[1], sum(width for _, _, width in parts)))
    target = 0
    for pieces, start, width in parts:
        for array, index, device in pieces:
            rows = array.shape[1]
            weight.add(array, index, rows, device * rows, start, width, target)
        target += width
    return weight


def gather(shard):
    every = lax.all_gather(shard, BOTH, axis=0)
    return [(every, i, i) for i in range(every.shape[0])]


class Gather:
    def __init__(self, grid, shard):
        self.grid = grid
        if not grid.cube:
            self.all = gather(shard)
            return
        shard = shard[None]
        self.got = [shard] + [grid.along_z(shard, k) for k in range(1, grid.nz)]

    def near(self, clock, wait):
        if not self.grid.cube:
            return wait
        own = jnp.concatenate(self.got)
        own, wait = clock(own, wait)
        self.got = [own, self.grid.over_xy(own), self.grid.over_x(own), self.grid.over_y(own)]
        return wait

    def pieces(self, clock):
        grid = self.grid
        if not grid.cube:
            return self.all
        self.got = clock(*self.got)
        pieces = []
        for (y, x), piece in zip(((0, 0), (1, 1), (0, 1), (1, 0)), self.got):
            for c, array in enumerate((piece, grid.over_core(piece))):
                pieces += [(array, k, grid.device(c, y, x, k)) for k in range(grid.nz)]
        return pieces


class Clock:
    def __init__(self):
        self.token = None

    def __call__(self, *values):
        if self.token is None:
            self.token = jnp.zeros((8, 128), F32)
        *values, self.token = lax.optimization_barrier((*values, self.token))
        return values[0] if len(values) == 1 else values


def run(kernel, weights, ins, outs, steps, flops, scratch=(), scalars=(), name=None, share=SHORT, stages=1):
    rows_at = [row for w in weights for row in w.rows_at] + list(scalars)
    rows_at = jnp.stack([jnp.asarray(row, jnp.int32) for row in rows_at] or [jnp.int32(0)])
    moves = []
    for which, w in enumerate(weights):
        cut = w.shape[1] // stages
        for n, (i, index, rows, source, width, target) in enumerate(w.copies):
            at = target
            while at < target + width:
                size = min(cut - at % cut, target + width - at)
                moves.append((at // cut, which, n, (i, index, rows, source + at - target, size, at)))
                at += size
    moves.sort(key=lambda move: move[0])
    bases = [sum(len(w.copies) for w in weights[:j]) for j in range(len(weights))]
    n_copies = sum(len(w.copies) for w in weights)
    n_pieces = [len(w.arrays) for w in weights]

    def body(at, *refs):
        refs = list(refs)

        def take(count):
            taken, refs[:count] = refs[:count], []
            return taken

        piece_refs = [take(count) for count in n_pieces]
        in_refs, out_refs = take(len(ins)), take(len(outs))
        held = take(len(weights))
        sems = take(1)[0] if moves else None

        def copies(stage=None):
            for n, (due, which, row, (i, index, rows, source, width, target)) in enumerate(moves):
                if stage is None or due == stage:
                    ref = piece_refs[which][i] if index is None else piece_refs[which][i].at[index]
                    yield pltpu.make_async_copy(
                        ref.at[:, pl.ds(source, width)],
                        held[which].at[pl.ds(pl.multiple_of(at[bases[which] + row], rows), rows), pl.ds(target, width)],
                        sems.at[n],
                    )

        step = pl.program_id(0)
        if moves:

            @pl.when(step == 0)
            def _():
                for copy in copies():
                    copy.start()

            for stage in range(stages):

                @pl.when(step == stage * (steps // stages))
                def _():
                    for copy in copies(stage):
                        copy.wait()

        values = [at[n_copies + i] for i in range(len(scalars))]
        kernel(values, in_refs, out_refs, held, refs)

    anywhere = pl.BlockSpec(memory_space=pl.ANY)

    def spec(block, index):
        if index is shifted_row_block:
            return pl.BlockSpec(block, lambda i, at: (at[n_copies] + i, 0))
        if index is shifted_part_block:
            return pl.BlockSpec(block, lambda i, at: (0, at[n_copies] + i, 0))
        return pl.BlockSpec(block, lambda i, at: index(i))

    semaphores = [pltpu.SemaphoreType.DMA((len(moves),))] if moves else []
    return pl.pallas_call(
        body,
        grid_spec=pltpu.PrefetchScalarGridSpec(
            num_scalar_prefetch=1,
            grid=(steps,),
            in_specs=[anywhere] * sum(n_pieces) + [spec(block, index) for _, block, index in ins],
            out_specs=[spec(block, index) for _, _, block, index in outs],
            scratch_shapes=[pltpu.VMEM(w.shape, BF) for w in weights] + semaphores + list(scratch),
        ),
        out_shape=[jax.ShapeDtypeStruct(shape, dtype) for shape, dtype, _, _ in outs],
        compiler_params=pltpu.CompilerParams(vmem_limit_bytes=VMEM_BYTES),
        name=name,
        cost_estimate=cost(flops * share),
    )(rows_at, *[a for w in weights for a in w.arrays], *[a for a, _, _ in ins])


def pick(array, index, axis):
    return lax.dynamic_index_in_dim(array, index, axis, keepdims=False)


def total(terms):
    value = terms[0].astype(F32)
    for term in terms[1:]:
        value = value + term.astype(F32)
    return value


def split_sum(terms, order, name, share):
    parts, size = terms[0].shape[0], terms[0].size
    rest = terms[0].shape[1:]
    columns = terms[0].shape[-1]
    rows = size // parts // columns
    tile = rows
    limit = min(2**19, max(2**17, rows * columns // 2))
    while tile * columns > limit and tile % 32 == 0:
        tile //= 2
    flat = [t.reshape(parts, rows, columns) for t in terms]
    wanted = len(order)

    def kernel(at, *refs):
        del at
        for j in range(wanted):
            value = refs[j][0].astype(F32)
            for i in range(1, len(terms)):
                value = value + refs[i * wanted + j][0].astype(F32)
            refs[len(terms) * wanted + j][...] = value.astype(terms[0].dtype)

    outs = pl.pallas_call(
        kernel,
        grid_spec=pltpu.PrefetchScalarGridSpec(
            num_scalar_prefetch=1,
            grid=(rows // tile,),
            in_specs=[
                pl.BlockSpec((1, tile, columns), lambda i, at, j=j: (at[j], i, 0))
                for _ in terms
                for j in range(wanted)
            ],
            out_specs=[pl.BlockSpec((tile, columns), lambda i, at: (i, 0))] * wanted,
        ),
        out_shape=[jax.ShapeDtypeStruct((rows, columns), terms[0].dtype)] * wanted,
        compiler_params=pltpu.CompilerParams(vmem_limit_bytes=VMEM_BYTES),
        name=name,
        cost_estimate=cost(2e10 * share),
    )(jnp.stack(order).astype(jnp.int32), *[t for t in flat for _ in range(wanted)])
    return [out.reshape(rest) for out in outs]


class Scatter:
    def __init__(self, grid, clock, kept, sent, order):
        self.grid, self.clock, self.order = grid, clock, order
        self.own, self.got = [kept], [grid.over_core(sent)]

    def step(self, share=SHORT):
        grid, axis, self.order = self.grid, self.order[0], self.order[1:]
        terms = self.clock(*self.own, *self.got)
        if axis == "z":
            places = [(grid.z + k) % grid.nz for k in range(grid.nz)]
            own, *parts = self.clock(*split_sum(terms, places, SUM + axis, share))
            self.got = [grid.along_z(part, k) for k, part in enumerate(parts, 1)]
        else:
            mine, move = (grid.y, grid.over_y) if axis == "y" else (grid.x, grid.over_x)
            own, part = self.clock(*split_sum(terms, [mine, 1 - mine], SUM + axis, share))
            self.got = [move(part)]
        self.own = [own]

    def wait(self, clock):
        if self.got:
            self.got = list(clock(*self.got))

    def result(self):
        return total(self.own + self.got)


class Summed:
    def __init__(self, value):
        self.value, self.own = value, []

    def step(self, share=SHORT):
        pass

    def wait(self, clock):
        pass

    def result(self):
        return lax.psum_scatter(self.value, BOTH, scatter_dimension=0, tiled=True)


def to_whole(grid, part):
    group, count = grid.group, part.shape[0]
    if group == 1:
        return part
    place = lax.axis_index(SEQ)
    if group == 2 and count == 2:
        kept, got = pick(part, place, 0), grid.over_x(pick(part, 1 - place, 0))
        first = jnp.where(place == 0, kept, got)
        second = jnp.where(place == 0, got, kept)
        return jnp.concatenate([first, second])[None]
    if count % group == 0:
        return lax.all_to_all(part, SEQ, split_axis=0, concat_axis=1, tiled=True)
    every = lax.all_gather(part, SEQ, axis=1, tiled=True)
    return pick(every, place % count, 0)[None]


class FromWhole:
    def __init__(self, grid, clock, whole, count):
        self.grid, self.clock, self.whole, self.count = grid, clock, whole, count
        self.swap = grid.group == 2 and count == 2
        if self.swap:
            place = lax.axis_index(SEQ)
            halves = whole.reshape(2, -1, whole.shape[-1])
            self.kept, self.got = pick(halves, place, 0), grid.over_x(pick(halves, 1 - place, 0))

    def result(self):
        group, whole, count = self.grid.group, self.whole, self.count
        place = lax.axis_index(SEQ)
        if self.swap:
            got = self.clock(self.got)
            return jnp.stack([jnp.where(place == 0, self.kept, got), jnp.where(place == 0, got, self.kept)])
        if group == 1:
            return whole
        if count % group == 0:
            return lax.all_to_all(whole, SEQ, split_axis=1, concat_axis=0, tiled=True)
        every = lax.all_gather(whole[0], SEQ, axis=0)[:count]
        rows = whole.shape[1] // group
        return lax.dynamic_slice_in_dim(every, place * rows, rows, 1)


def attention_forward_kernel(
    q_ref, k_ref, v_ref, mask_ref, out_ref, total_ref, weight_ref, *, head, chunk
):
    factor = head**-0.5 * math.log2(math.e)
    rows = q_ref.shape[1]
    for h in range(q_ref.shape[2] // head):
        lanes = slice(h * head, (h + 1) * head)
        keys, values = k_ref[0, :, lanes], v_ref[0, :, lanes]
        for start in range(0, rows, chunk):
            part = slice(start, start + chunk)
            scores = dot(keys, q_ref[0, part, lanes], NT)
            weights = jnp.exp2(scores * factor + mask_ref[0, :, part])
            total = jnp.sum(weights, axis=0, keepdims=True)
            low = weights.astype(BF)
            weight_ref[0, 0, h, :, part] = low
            summed = dot(values, low, TN)
            total_ref[0, 0, h : h + 1, part] = total
            out_ref[0, part, lanes] = (summed / total).T.astype(BF)


def attention_backward_kernel(
    q_ref, k_ref, v_ref, weight_ref, grad_ref, ctx_ref, total_ref, out_ref, dk_sum, dv_sum, *, head, chunk
):
    scale = head**-0.5
    rows = q_ref.shape[1]
    for h in range(q_ref.shape[2] // head):
        lanes = slice(h * head, (h + 1) * head)
        keys, values = k_ref[0, :, lanes], v_ref[0, :, lanes]
        keys_t = keys.T
        for start in range(0, rows, chunk):
            part = slice(start, start + chunk)
            queries = q_ref[0, part, lanes]
            low = weight_ref[0, 0, h, :, part]
            inverse = 1.0 / total_ref[0, 0, h : h + 1, part]
            grad = grad_ref[0, part, lanes].astype(F32)
            product = (grad * ctx_ref[0, part, lanes].astype(F32)).T
            grad_total = -jnp.sum(product, axis=0, keepdims=True) * inverse
            grad_summed = (grad.T * inverse).astype(BF)
            grad_probs = dot(values, grad_summed)
            grad_scores = (low.astype(F32) * (grad_probs + grad_total)).astype(BF)
            dv_part = dot(low, grad_summed, NT)
            dk_part = dot(grad_scores, queries)
            if start == 0:
                dv_sum[...] = dv_part
                dk_sum[...] = dk_part
            else:
                dv_sum[...] += dv_part
                dk_sum[...] += dk_part
            out_ref[0, 0, part, lanes] = (dot(keys_t, grad_scores).T * scale).astype(BF)
        out_ref[1, 0, :, lanes] = (dk_sum[...] * scale).astype(BF)
        out_ref[2, 0, :, lanes] = dv_sum[...].astype(BF)


def attention_specs(length, width, group):
    head = width // HEADS
    lanes = max(128, head)
    steps = width // lanes // GROUPS

    def columns(which):
        return pl.BlockSpec((1, length, lanes), lambda b, p: (b, 0, (which * GROUPS + group) * steps + p))

    own = pl.BlockSpec((1, length, lanes), lambda b, p: (b, 0, p))
    mask = pl.BlockSpec((1, length, length), lambda b, p: (b, 0, 0))
    totals = pl.BlockSpec((1, 1, lanes // head, length), lambda b, p: (b, p, 0, 0))
    weights = pl.BlockSpec((1, 1, lanes // head, length, length), lambda b, p: (b, p, 0, 0, 0))
    return head, lanes, steps, columns, own, mask, totals, weights


def attention_forward(qkv, mask, group):
    count, length, width = qkv.shape
    width = width // 3
    head, lanes, steps, columns, own, mask_spec, totals, weights = attention_specs(length, width, group)
    return pl.pallas_call(
        partial(attention_forward_kernel, head=head, chunk=512),
        grid=(count, steps),
        in_specs=[columns(0), columns(1), columns(2), mask_spec],
        out_specs=[own, totals, weights],
        out_shape=[
            jax.ShapeDtypeStruct((count, length, width // GROUPS), BF),
            jax.ShapeDtypeStruct((count, steps, lanes // head, length), F32),
            jax.ShapeDtypeStruct((count, steps, lanes // head, length, length), BF),
        ],
        name="attention_forward",
        compiler_params=pltpu.CompilerParams(vmem_limit_bytes=VMEM_BYTES),
        cost_estimate=cost(12 * count * length * length * width // GROUPS),
    )(qkv, qkv, qkv, mask)


def attention_backward(qkv, grad, context, totals_in, weights_in, group):
    count, length, width = grad.shape
    head, lanes, steps, columns, own, mask_spec, totals, weights = attention_specs(length, width, group)
    grads = pl.BlockSpec((3, 1, length, lanes), lambda b, p: (0, b, 0, p))
    return pl.pallas_call(
        partial(attention_backward_kernel, head=head, chunk=256),
        grid=(count, steps),
        in_specs=[columns(0), columns(1), columns(2), weights, columns(0), own, totals],
        out_specs=grads,
        out_shape=jax.ShapeDtypeStruct((3, count, length, width // GROUPS), BF),
        scratch_shapes=[pltpu.VMEM((length, head), F32)] * 2,
        name="attention_backward",
        compiler_params=pltpu.CompilerParams(vmem_limit_bytes=VMEM_BYTES),
        cost_estimate=cost(26 * count * length * length * width * (LONG if group else SHORT)),
    )(qkv, qkv, qkv, weights_in, grad, context, totals_in)


def attention_mask(segments, globals_pair, randoms):
    count, blocks = randoms.shape[:2]
    length = segments.shape[1]
    numbers = jnp.arange(blocks, dtype=jnp.int32)
    chosen = jnp.any(globals_pair[:, :, None] == numbers, axis=1)
    nearby = jnp.abs(numbers[:, None] - numbers[None, :]) <= 1
    picked = jnp.any(randoms[:, :, :, None] == numbers, axis=2)
    seen = chosen[:, :, None] | chosen[:, None, :] | nearby[None] | picked
    seen = jnp.swapaxes(seen, 1, 2)[:, :, None, :, None]
    seen = jnp.broadcast_to(seen, (count, blocks, BLK, blocks, BLK)).reshape(count, length, length)
    same = segments[:, :, None] == segments[:, None, :]
    return jnp.where(seen & same, 0.0, MASKED).astype(F32)


def normalise(values):
    centred = values - jnp.mean(values, -1, keepdims=True)
    inverse = lax.rsqrt(jnp.mean(centred * centred, -1, keepdims=True) + EPSILON)
    return centred * inverse, inverse


def normalise_back(grad, values, gain):
    unit, inverse = normalise(values)
    inner = grad * gain
    grad_in = inverse * (
        inner - jnp.mean(inner, -1, keepdims=True) - unit * jnp.mean(inner * unit, -1, keepdims=True)
    )
    return grad_in, jnp.sum(grad * unit, 0, keepdims=True), jnp.sum(grad, 0, keepdims=True)


def accumulate(ref, rows):
    first = pl.program_id(0) == 0
    for j, row in enumerate(rows):

        @pl.when(first)
        def _():
            ref[j : j + 1] = row

        @pl.when(jnp.logical_not(first))
        def _():
            ref[j : j + 1] += row


def row_block(i):
    return (i, 0)


def shifted_row_block(i):
    raise NotImplementedError


def shifted_part_block(i):
    raise NotImplementedError


def fixed_block(i):
    return (0, 0)


def column_block(i):
    return (0, i)


def project_in(x, w_qkv, extra):
    rows, width = x.shape

    def kernel(_, ins, outs, weights, scratch):
        qkv, turned, params = outs
        w, small = weights

        @pl.when(pl.program_id(0) == 0)
        def _():
            params[...] = small[...].astype(F32).T[:16]

        unit, _ = normalise(ins[0][...].astype(F32))
        normed = (unit * params[0:1] + params[1:2]).astype(BF)
        turned[...] = normed.T
        for part, bias in enumerate((params[2:3], None, params[3:4])):
            columns = slice(part * width, (part + 1) * width)
            value = dot(normed, w[:, columns])
            qkv[:, columns] = (value if bias is None else value + bias).astype(BF)

    return run(
        kernel,
        [w_qkv, extra],
        [(x, (TILE, width), row_block)],
        [
            ((rows, 3 * width), BF, (TILE, 3 * width), row_block),
            ((width, rows), BF, (width, TILE), column_block),
            ((16, width), F32, (16, width), fixed_block),
        ],
        rows // TILE,
        6 * rows * width * width,
        name="project_in",
    )


def project_out(contexts, x, params, w_o):
    rows, width = x.shape

    def kernel(_, ins, outs, weights, scratch):
        x_ref, params = ins[:2]
        residual, normed, turned, context_turned = outs
        parts = [ref[...] for ref in ins[2:]]
        context = jnp.concatenate(parts, axis=1)
        context_turned[...] = context.T
        value = x_ref[...].astype(F32) + dot(context, weights[0][...]) + params[4:5]
        residual[...] = value
        unit, _ = normalise(value)
        low = (unit * params[5:6] + params[6:7]).astype(BF)
        normed[...] = low
        turned[...] = low.T

    return run(
        kernel,
        [w_o],
        [(x, (TILE, width), row_block), (params, (16, width), fixed_block)]
        + [(c, (TILE, c.shape[1]), row_block) for c in contexts],
        [
            ((rows, width), F32, (TILE, width), row_block),
            ((rows, width), BF, (TILE, width), row_block),
            ((width, rows), BF, (width, TILE), column_block),
            ((width, rows), BF, (width, TILE), column_block),
        ],
        rows // TILE,
        2 * rows * width * width,
        name="project_out",
    )


def feed_up(normed, w_up, bias):
    rows, width = normed.shape
    wide = w_up.shape[1]
    outer = math.sqrt(2 / math.pi)
    cubic = 0.044715

    tile = min(512, wide)

    def kernel(_, ins, outs, weights, scratch):
        value, slope = outs
        columns = pl.ds(pl.multiple_of(pl.program_id(0) * tile, tile), tile)
        u = dot(ins[0][...], weights[0][:, columns]) + ins[1][...]
        square = u * u
        half = 0.5 + 0.5 * jnp.tanh(u * (outer + outer * cubic * square))
        gelu = u * half
        value[...] = gelu.astype(BF)
        rest = gelu * (1.0 - half) * (2 * outer + 6 * outer * cubic * square)
        slope[...] = (half + rest).astype(BF)

    return run(
        kernel,
        [w_up],
        [(normed, (rows, width), fixed_block), (bias, (1, tile), column_block)],
        [((rows, wide), BF, (rows, tile), column_block)] * 2,
        wide // tile,
        2 * rows * width * wide,
        name="feed_up",
        stages=4,
    )


def feed_down(activated, slope, residual, upstream, params, w_down):
    rows, wide = activated.shape
    width = residual.shape[1]

    def kernel(_, ins, outs, weights, scratch):
        act, slope, residual, upstream, params = ins
        mixed, grad_hidden, sum_up, sum_down = outs
        w = weights[0]
        value = residual[...] + dot(act[...], w[...]) + params[7:8]
        mixed[...] = value.astype(BF)
        dy = upstream[...]
        sums = []
        for start in range(0, wide, width):
            columns = slice(start, start + width)
            grad = dot(dy, w[columns, :], NT).astype(BF).astype(F32)
            low = (grad * slope[:, columns].astype(F32)).astype(BF)
            grad_hidden[:, columns] = low
            sums.append(jnp.sum(low.astype(F32), 0, keepdims=True))
        accumulate(sum_up, [jnp.concatenate(sums, axis=1)])
        accumulate(sum_down, [jnp.sum(dy.astype(F32), 0, keepdims=True)])

    return run(
        kernel,
        [w_down],
        [
            (activated, (TILE, wide), row_block),
            (slope, (TILE, wide), row_block),
            (residual, (TILE, width), row_block),
            (upstream, (TILE, width), row_block),
            (params, (16, width), fixed_block),
        ],
        [
            ((rows, width), BF, (TILE, width), row_block),
            ((rows, wide), BF, (TILE, wide), row_block),
            ((8, wide), F32, (8, wide), fixed_block),
            ((8, width), F32, (8, width), fixed_block),
        ],
        rows // TILE,
        4 * rows * width * wide,
        name="feed_down",
        share=LONG,
    )


def feed_back(grad_hidden, residual, upstream, params, w_up, w_o):
    rows, width = residual.shape
    wide = grad_hidden.shape[1]

    def kernel(_, ins, outs, weights, scratch):
        du, residual, upstream, params = ins
        grad_residual, grad_att, grad_context, sums = outs
        grad = dot(du[...], weights[0][...], NT)
        part, gain, shift = normalise_back(grad, residual[...], params[5:6])
        total = upstream[...].astype(F32) + part
        grad_residual[...] = total
        low = total.astype(BF)
        grad_att[...] = low
        grad_context[...] = dot(low, weights[1][...], NT).astype(BF)
        accumulate(sums, [jnp.sum(low.astype(F32), 0, keepdims=True), gain, shift])

    return run(
        kernel,
        [w_up, w_o],
        [
            (grad_hidden, (TILE, wide), row_block),
            (residual, (TILE, width), row_block),
            (upstream, (TILE, width), row_block),
            (params, (16, width), fixed_block),
        ],
        [
            ((rows, width), F32, (TILE, width), row_block),
            ((rows, width), BF, (TILE, width), row_block),
            ((rows, width), BF, (TILE, width), row_block),
            ((8, width), F32, (8, width), fixed_block),
        ],
        rows // TILE,
        2 * rows * width * (wide + width),
        name="feed_back",
        share=LONG,
    )


def project_back(grads, grad_residual, x, params, w_qkv, first, count):
    width = x.shape[1]
    each = width // GROUPS

    def kernel(_, ins, outs, weights, scratch):
        grad_residual, x_ref, params = ins[:3]
        grad_in, sums = outs
        w = weights[0]
        grad = None
        biases = []
        for part in range(3):
            cut = [ref[part] for ref in ins[3:]]
            low = jnp.concatenate(cut, axis=1)
            if part != 1:
                biases.append(jnp.sum(low.astype(F32), 0, keepdims=True))
            value = dot(low, w[:, part * width : (part + 1) * width], NT)
            grad = value if grad is None else grad + value
        part, gain, shift = normalise_back(grad, x_ref[...].astype(F32), params[0:1])
        grad_in[...] = (grad_residual[...] + part).astype(BF)
        accumulate(sums, [gain, shift] + biases)

    return run(
        kernel,
        [w_qkv],
        [
            (grad_residual, (TILE, width), shifted_row_block),
            (x, (TILE, width), shifted_row_block),
            (params, (16, width), fixed_block),
        ]
        + [(g, (3, TILE, each), shifted_part_block) for g in grads],
        [
            ((count * TILE, width), BF, (TILE, width), row_block),
            ((8, width), F32, (8, width), fixed_block),
        ],
        count,
        6 * count * TILE * width * width,
        scalars=[first],
        name="project_back",
    )


def weight_grad(grid, clock, pairs, order):
    if not grid.cube:
        return Summed(jnp.concatenate([dot(turned, part) for turned, right in pairs for part in right], axis=1))
    features, rows = pairs[0][0].shape
    tile = min(512, *(right.shape[2] for _, right in pairs))
    counts = [right.shape[0] * right.shape[2] // tile for _, right in pairs]
    columns = sum(counts) * tile
    shard = features // grid.nz // 8
    places, shape = leading(grid, order)

    def kernel(scalars, ins, outs, weights, scratch):
        first = scalars[0] == 0
        step = pl.program_id(0)

        def work(turned, right, low, high):
            value = dot(turned[...], right[0]).astype(BF)
            for (z, y, x), at in places:
                start = ((z * 2 + y) * 4 + x) * shard
                low[at * shard : (at + 1) * shard] = value[start : start + shard]
                start += 2 * shard
                high[at * shard : (at + 1) * shard] = value[start : start + shard]

        done = 0
        for j, count in enumerate(counts):
            here = (step >= done) & (step < done + count)
            done += count

            @pl.when(here & first)
            def _():
                work(ins[2 * j], ins[2 * j + 1], *outs)

            @pl.when(here & jnp.logical_not(first))
            def _():
                work(ins[2 * j], ins[2 * j + 1], outs[1], outs[0])

    ins, done = [], 0
    for (turned, right), count in zip(pairs, counts):
        per = right.shape[2] // tile

        def block(i, done=done, count=count, per=per):
            j = jnp.clip(i - done, 0, count - 1)
            return (j // per, 0, j % per)

        turned, right = clock(turned, right)
        ins += [(turned, (features, rows), fixed_block), (right, (1, rows, tile), block)]
        done += count
    kept, sent = run(
        kernel,
        [],
        ins,
        [((features // 2, columns), BF, (features // 2, tile), column_block)] * 2,
        sum(counts),
        2 * rows * features * columns,
        scalars=[grid.core],
        name=WG + str(columns),
    )
    shape += (shard, columns)
    kept, sent = clock(kept, sent)
    return Scatter(grid, clock, kept.reshape(shape), sent.reshape(shape), order)


def weight_grad_turned(grid, clock, left, right, order):
    rows, features = left.shape
    each = right.shape[1] // (grid.nz * 8)
    places, shape = leading(grid, order)

    def kernel(scalars, ins, outs, weights, scratch):
        first = scalars[0] == 0
        value = dot(ins[0][...], ins[1][...], TN).astype(BF)

        def store(low, high):
            for (z, y, x), at in places:
                start = ((z * 2 + y) * 4 + x) * each
                low[at] = value[:, start : start + each]
                start += 2 * each
                high[at] = value[:, start : start + each]

        @pl.when(first)
        def _():
            store(*outs)

        @pl.when(jnp.logical_not(first))
        def _():
            store(outs[1], outs[0])

    tile = min(256, features)
    shape += (features, each)
    left, right = clock(left, right)
    kept, sent = run(
        kernel,
        [],
        [(left, (rows, tile), column_block), (right, right.shape, fixed_block)],
        [((grid.nz * 4, features, each), BF, (grid.nz * 4, tile, each), lambda i: (0, i, 0))] * 2,
        features // tile,
        2 * rows * features * right.shape[1],
        scalars=[grid.core],
        name=WG + "turned",
    )
    kept, sent = clock(kept, sent)
    return Scatter(grid, clock, kept.reshape(shape), sent.reshape(shape), order)


def leading(grid, order):
    counts = {"z": grid.nz, "y": 2, "x": 2}
    places = []
    for z in range(grid.nz):
        for y in range(2):
            for x in range(2):
                here = {"z": z, "y": y, "x": x}
                at = 0
                for axis in order:
                    at = at * counts[axis] + here[axis]
                places.append(((z, y, x), at))
    return places, tuple(counts[axis] for axis in order)


def shards(tokens, cotangent, segments, global_blocks, random_blocks, *params):
    grid = Grid()
    gain1, shift1, w_q, b_q, w_k, w_v, b_v, w_o, b_o, gain2, shift2, w_up, b_up, w_down, b_down = params
    count = tokens.shape[0]
    width = tokens.shape[-1]
    wide = w_up.shape[1]
    each = w_v.shape[0]
    devices = grid.dp * grid.group
    replicas = max(1, grid.group // count)

    inputs = to_whole(grid, tokens)
    n, length = inputs.shape[:2]
    rows = n * length
    inputs = inputs.reshape(rows, width)
    vectors = [gain1, shift1, b_q, b_v, b_o, gain2, shift2, b_down]
    extra = jnp.concatenate([*vectors, b_up]).reshape(-1, each).T
    extra = jnp.pad(extra, ((0, 0), (0, 128 - extra.shape[1])))

    clock = Clock()
    first = gather(jnp.concatenate([w_q, w_k], axis=1))
    second = Gather(grid, jnp.concatenate([w_v, w_o, extra], axis=1))
    inputs = second.near(clock, inputs)
    third = Gather(grid, clock(w_up))
    fourth = gather(w_down)
    if grid.group > 1:
        place = lax.axis_index(SEQ)
        start = place * n if count % grid.group == 0 else place % count
        segments, global_blocks, random_blocks = (
            lax.dynamic_slice_in_dim(a, start, n, 0) for a in (segments, global_blocks, random_blocks)
        )
    mask = attention_mask(segments, global_blocks, random_blocks)

    second = second.pieces(clock)
    inputs = third.near(clock, inputs)
    w_qkv = columns_of((first, 0, 2 * width), (second, 0, width))
    w_o, extra = columns_of((second, width, width)), columns_of((second, 2 * width, 128))
    inputs = clock(inputs)
    qkv, normed1_turned, params = clock(*project_in(inputs, w_qkv, extra))
    qkv = qkv.reshape(n, length, 3 * width)
    upstream = to_whole(grid, clock(cotangent)).reshape(rows, width)
    attended = []
    for g in range(GROUPS):
        qkv, mask = clock(qkv, mask)
        attended.append(clock(*attention_forward(qkv, mask, g)))
    contexts = [a[0].reshape(rows, -1) for a in attended]
    contexts[0] = clock(contexts[0])
    residual, normed2, normed2_turned, context_turned = clock(*project_out(contexts, inputs, params, w_o))
    w_up, w_down = columns_of((third.pieces(clock), 0, wide)), columns_of((fourth, 0, width))
    normed2 = clock(normed2)
    bias_up = params[8 : 8 + wide // width].reshape(-1, devices, each).transpose(1, 0, 2).reshape(1, -1)
    activated, slope = clock(*feed_up(normed2, w_up, bias_up))

    if grid.cube:
        sum_w_down = weight_grad_turned(grid, clock, upstream, activated, "yzx")
    else:
        sum_w_down = Summed(dot(activated, upstream, TN))
    activated = clock(activated)
    mixed, grad_hidden, sum_up, sum_down = clock(
        *feed_down(activated, slope, residual, upstream, params, w_down)
    )
    mixed = FromWhole(grid, clock, mixed.reshape(n, length, width), count)
    sum_w_down.step()
    sum_w_up = weight_grad(grid, clock, [(normed2_turned, grad_hidden[None])], "xyz")
    grad_hidden = clock(grad_hidden)
    grad_residual, grad_att, grad_context, sums2 = clock(
        *feed_back(grad_hidden, residual, upstream, params, w_up, w_o)
    )
    mixed = mixed.result()
    sum_w_up.step()
    sum_w_down.step()
    grad_context = grad_context.reshape(n, length, width)
    grads, sums_qkv = [], []
    for g in range(GROUPS):
        grad_context = clock(grad_context)
        grad = clock(attention_backward(qkv, grad_context, *attended[g], g)).reshape(3, rows, -1)
        grads.append(grad)
        if g > 0:
            sum_w_up.step()
            sums_qkv[0].step()
        pairs = [(normed1_turned, grad)] + [(context_turned, grad_att[None])] * (g == 0)
        sums_qkv.append(weight_grad(grid, clock, pairs, "yxz"))
        if g == 0:
            sum_w_down.step()
            sum_w_up.step()
    sums_qkv[1].step()
    steps = rows // TILE
    grads[-1] = clock(grads[-1])
    grad_inputs, sums1 = clock(*project_back(grads, grad_residual, inputs, params, w_qkv, 0, steps))
    sum_w_up.wait(clock)
    sums_qkv[0].step()
    sums_qkv[1].step()
    grad_inputs = clock(grad_inputs)
    grad_inputs = FromWhole(grid, clock, grad_inputs.reshape(n, length, width), count)
    vectors = jnp.concatenate([sums1[:4], sums2[:3], sum_down[:1]])
    vectors = vectors.reshape(8, devices, each).transpose(1, 0, 2).reshape(devices, -1)
    vectors = jnp.concatenate([vectors, sum_up[:1].reshape(devices, -1)], axis=1)
    if grid.cube:
        vectors = halve(clock(vectors).reshape(grid.nz, 2, 2, 2, -1, 128), grid.core, 2, grid.over_core)
    sums_qkv[1].step(LONG)
    sums_qkv[0].step()
    if grid.cube:
        vectors = halve(clock(vectors), grid.y, 1, grid.over_y)
    grad_inputs = grad_inputs.result()
    if grid.cube:
        sums_qkv[1].wait(clock)
        vectors = halve(clock(vectors), grid.x, 1, grid.over_x)
        sums_qkv[0].wait(clock)
        parts = [pick(vectors, (grid.z + k) % grid.nz, 0) for k in range(grid.nz)]
        vectors = total(parts[:1] + [grid.along_z(part, k) for k, part in enumerate(parts) if k])
    else:
        vectors = lax.psum_scatter(vectors, BOTH, scatter_dimension=0, tiled=True)
    vectors = vectors + clock.token[0, 0]

    share = 1.0 / replicas
    grad_w_down = sum_w_down.result() * share
    if grid.cube:
        grad_w_down = grad_w_down.T
    grad_w_up = sum_w_up.result() * share
    ended = [moving.result() * share for moving in sums_qkv]
    cut = width // GROUPS
    grad_w_o = ended[0][:, 3 * cut :]
    grad_w_q, grad_w_k, grad_w_v = (
        jnp.concatenate([e[:, j * cut : (j + 1) * cut] for e in ended], axis=1) for j in range(3)
    )
    vectors = (vectors * share).reshape(-1)
    grad_b_up = vectors[8 * each :]
    grad_gain1, grad_shift1, grad_b_q, grad_b_v, grad_b_o, grad_gain2, grad_shift2, grad_b_down = (
        vectors[j * each : (j + 1) * each] for j in range(8)
    )
    return (
        mixed, grad_inputs, grad_gain1, grad_shift1, grad_w_q, grad_b_q, grad_w_k, grad_w_v, grad_b_v,
        grad_w_o, grad_b_o, grad_gain2, grad_shift2, grad_w_up, grad_b_up, grad_w_down, grad_b_down,
    )


def halve(value, mine, dim, move):
    return pick(value, mine, dim) + move(pick(value, 1 - mine, dim))


def solution(mesh):
    rows = P(DP, SEQ, None)
    vector, matrix = P(BOTH), P(BOTH, None)
    params = (
        vector, vector, matrix, vector, matrix, matrix, vector, matrix, vector, vector, vector, matrix,
        vector, matrix, vector,
    )
    in_specs = (rows, rows, P(DP, None), P(DP, None), P(DP, None, None)) + params
    out_specs = (rows, rows) + params
    return jax.shard_map(shards, mesh=mesh, in_specs=in_specs, out_specs=out_specs, check_vma=False)
```
